32 devices in a mesh: parts: 2 (over y), row: 16 (over z, x, core).
Axes of the slice: x: 2, y: 2, z: 4, core: 2. Of those that a mesh axis runs over, the one named last changes fastest.
Arguments:
- node_latent: bfloat16 [32768, 256], P(('parts', 'row')), parts along dimension 0, may hold values from -120 to 120
- agg_saved: bfloat16 [32768, 256], P(('parts', 'row')), parts along dimension 0, may hold values from -12 to 12
- node_cot: bfloat16 [32768, 256], P(('parts', 'row')), parts along dimension 0, may hold values from -6 to 6
- edge_latent: bfloat16 [24576, 256], P(('parts', 'row')), parts along dimension 0, may hold values from -120 to 120
- edge_cot: bfloat16 [24576, 256], P(('parts', 'row')), parts along dimension 0, may hold values from -6 to 6
- send_local: int32 [192, 128], P(('parts', 'row')), parts along dimension 0, may hold values from 0 to 1023
- recv_local: int32 [192, 128], P(('parts', 'row')), parts along dimension 0, may hold values from 0 to 1023
- send_slot: int32 [192], P(('parts', 'row')), parts along dimension 0, may hold values from 0 to 2, as said below
- recv_slot: int32 [192], P(('parts', 'row')), parts along dimension 0, may hold values from 0 to 2, as said below
- tile_count: int32 [32], P(('parts', 'row')), parts along dimension 0, may hold values from 3 to 6, as said below
- edge_w_in: bfloat16 [768, 256], replicated, may hold values from -0.21875 to 0.21875
- edge_w_out: bfloat16 [256, 256], replicated, may hold values from -0.375 to 0.375
- edge_gain: float32 [256], replicated, may hold values from 0.1 to 1.9
- node_w_in: bfloat16 [512, 256], replicated, may hold values from -0.25 to 0.25
- node_w_out: bfloat16 [256, 256], replicated, may hold values from -0.375 to 0.375
- node_gain: float32 [256], replicated, may hold values from 0.1 to 1.9
Outputs:
- node_grad: bfloat16 [32768, 256], P(('parts', 'row')), parts along dimension 0
- edge_grad: bfloat16 [24576, 256], P(('parts', 'row')), parts along dimension 0
- edge_grad_w_in: float32 [1536, 256], P('parts'), parts along dimension 0
- edge_grad_w_out: float32 [512, 256], P('parts'), parts along dimension 0
- edge_grad_gain: float32 [512], P('parts'), parts along dimension 0
- node_grad_w_in: float32 [1024, 256], P('parts'), parts along dimension 0
- node_grad_w_out: float32 [512, 256], P('parts'), parts along dimension 0
- node_grad_gain: float32 [512], P('parts'), parts along dimension 0
The draws below stay inside these ranges and needn't reach their ends.
There are 2 independent parts, one for each index of `parts`. The reference program is written for one: setup_inputs(seed, part) draws one part's arguments, and reference() takes and returns one part's arrays. A program takes and returns all parts, laid end to end along the dimension named above; an argument that names none is the same for every part. Nothing has to cross between parts.
Inputs may be any that keep to these rules, and one draw needn't show every extreme that they name: Tiles 0 to tile_count - 1 of a device hold edges, its other tile slots are padding; some device has all 6 live. `send_slot`: on every device, the first 3 tiles name each sender block once. `recv_slot`: on every device, the first 3 tiles name each receiver block once.
All inputs are finite; a program needn't handle non-finite values.
Results may differ from the reference program's by a relative error of at most 0.0056.
Values may be sent and summed in bfloat16 or wider, within the bound.
A program may use at most 128 MiB of HBM per device.

```python
import math
import jax
import jax.numpy as jnp
from jax import lax

H = 256
NB = 1024
TILES = 6
TILE = 128
SLOTS = 3
STRIDE = 2
NODES = 16384
TILE_ROWS = 96
EDGES = 12288
N_ROW = 16


def row_scales(key, rows, top):
    return jnp.exp(jax.random.uniform(key, (rows, 1), jnp.float32) * math.log(top))


def latent_rows(key, rows, features):
    base_key, row_key = jax.random.split(key, 2)
    base_values = jax.random.normal(base_key, (rows, features), jnp.float32)
    values = jnp.clip(base_values, -6.0, 6.0) * row_scales(row_key, rows, 10.0)
    return values.astype(jnp.bfloat16)


def slot_table(key):
    device_key, tile_key = jax.random.split(key)
    rotation = jax.random.randint(device_key, (N_ROW, 1), 0, SLOTS)
    position = jnp.arange(TILES, dtype=jnp.int32)[None, :]
    leading = (position + rotation) % SLOTS
    others = jax.random.randint(tile_key, (N_ROW, TILES), 0, SLOTS)
    return jnp.where(position < SLOTS, leading, others).reshape(-1).astype(jnp.int32)


def draw_node_latent(key, part):
    key = jax.random.fold_in(key, 11)
    return latent_rows(key, NODES, H)


def draw_edge_latent(key, part):
    key = jax.random.fold_in(key, 12)
    return latent_rows(key, EDGES, H)


def draw_send_slot(key, part):
    key = jax.random.fold_in(key, 13)
    return slot_table(key)


def draw_recv_slot(key, part):
    key = jax.random.fold_in(key, 14)
    return slot_table(key)


def draw_tile_count(key, part):
    key = jax.random.fold_in(key, 15)
    first_key, second_key, order_key = jax.random.split(key, 3)
    extra_one = jax.random.randint(first_key, (N_ROW,), 0, TILES - SLOTS + 1)
    extra_two = jax.random.randint(second_key, (N_ROW,), 0, TILES - SLOTS + 1)
    counts = SLOTS + jnp.minimum(extra_one, extra_two)
    order = jax.random.permutation(order_key, N_ROW)
    counts = counts.at[order[0]].set(TILES)
    counts = counts.at[order[1]].set(SLOTS)
    return counts.astype(jnp.int32)


def set_ends(entries, own_key, least, high):
    longest = entries.shape.index(max(entries.shape))
    spots = []
    for shift in (0, 1):
        where = [jax.random.randint(jax.random.fold_in(own_key, axis), (), 0, length) for axis, length in enumerate(entries.shape)]
        where[longest] = (where[longest] + shift) % entries.shape[longest]
        spots.append(tuple(where))
    return entries.at[spots[0]].set(least).at[spots[1]].set(high)


def shard_levels(stream_key, dims, pieces, smallest, top_value):
    def one(dim, parts):
        steps = jax.random.uniform(jax.random.fold_in(jax.random.fold_in(stream_key, 6), dim), (parts,), jnp.float32, smallest / len(pieces), top_value / len(pieces))
        return jnp.repeat(jnp.exp(steps), dims[dim] // parts).reshape((-1,) + (1,) * (len(dims) - dim - 1))

    factor_of = one(*pieces[0])
    for cut in pieces[1:]:
        factor_of = factor_of * one(*cut)
    return factor_of


def noise(own_key, dims, spread, bound, pieces=(), held_as=jnp.bfloat16):
    factor_of = shard_levels(own_key, dims, pieces, -0.22, 0.18) if pieces else 1.0
    values = jax.random.normal(own_key, dims, jnp.float32) * spread * factor_of
    return jnp.minimum(jnp.maximum(values, -bound), bound).astype(held_as)


def setup_inputs(seed: int = 0, part: int = 0) -> dict:
    key_of = jax.random.split(jax.random.key(seed), 17)
    part_splits = jax.random.split(jax.random.fold_in(key_of[16], part), 17)
    return {
        "node_latent": draw_node_latent(jax.random.fold_in(jax.random.fold_in(key_of[16], part), 71), part),
        "agg_saved": noise(part_splits[1], (NODES, H), 2.0, 12.0, ((0, 16),)),
        "node_cot": noise(part_splits[2], (NODES, H), 1.0, 6.0, ((0, 16),)),
        "edge_latent": draw_edge_latent(jax.random.fold_in(jax.random.fold_in(key_of[16], part), 71), part),
        "edge_cot": noise(part_splits[4], (EDGES, H), 1.0, 6.0, ((0, 16),)),
        "send_local": set_ends(jax.random.randint(part_splits[5], (TILE_ROWS, TILE), 0, NB), jax.random.fold_in(part_splits[5], 1), 0, NB - 1).astype(jnp.int32),
        "recv_local": set_ends(jax.random.randint(part_splits[6], (TILE_ROWS, TILE), 0, NB), jax.random.fold_in(part_splits[6], 1), 0, NB - 1).astype(jnp.int32),
        "send_slot": draw_send_slot(jax.random.fold_in(jax.random.fold_in(key_of[16], part), 71), part),
        "recv_slot": draw_recv_slot(jax.random.fold_in(jax.random.fold_in(key_of[16], part), 71), part),
        "tile_count": draw_tile_count(jax.random.fold_in(jax.random.fold_in(key_of[16], part), 71), part),
        "edge_w_in": noise(key_of[10], (3 * H, H), (3 * H) ** -0.5, 0.21875),
        "edge_w_out": noise(key_of[11], (H, H), H ** -0.5, 0.375),
        "edge_gain": jnp.clip(1.0 + 0.18 * jax.random.normal(key_of[12], (H,), jnp.float32), 0.1, 1.9),
        "node_w_in": noise(key_of[13], (2 * H, H), (2 * H) ** -0.5, 0.25),
        "node_w_out": noise(key_of[14], (H, H), H ** -0.5, 0.375),
        "node_gain": jnp.clip(1.0 + 0.18 * jax.random.normal(key_of[15], (H,), jnp.float32), 0.1, 1.9),
    }


EPSILON = 1e-05

def mlp_backward(inputs, w_in, w_out, norm_gain, cotangent):
    preact = jnp.dot(inputs, w_in, preferred_element_type=jnp.float32)
    activation = jax.nn.silu(preact).astype(jnp.bfloat16)
    output = jnp.dot(activation, w_out, preferred_element_type=jnp.float32)
    row_mean = lax.optimization_barrier(jnp.mean(output, axis=-1, keepdims=True))
    centred = output - row_mean
    inverse = lax.rsqrt(lax.optimization_barrier(jnp.mean(centred * centred, axis=-1, keepdims=True)) + EPSILON)
    normed = centred * inverse
    grad_gain = lax.optimization_barrier(jnp.sum(cotangent * normed, axis=0))
    scaled = cotangent * norm_gain
    out_grad = inverse * (scaled - lax.optimization_barrier(jnp.mean(scaled, axis=-1, keepdims=True)) - normed * lax.optimization_barrier(jnp.mean(scaled * normed, axis=-1, keepdims=True)))
    out_grad = out_grad.astype(jnp.bfloat16)
    grad_w_out = jnp.dot(activation.T, out_grad, preferred_element_type=jnp.float32)
    sigmoid_pre = jax.nn.sigmoid(preact)
    act_grad = jnp.dot(out_grad, w_out.T, preferred_element_type=jnp.float32)
    pre_grad = (act_grad * sigmoid_pre * (1.0 + preact * (1.0 - sigmoid_pre))).astype(jnp.bfloat16)
    grad_w_in = jnp.dot(inputs.T, pre_grad, preferred_element_type=jnp.float32)
    in_grad = jnp.dot(pre_grad, w_in.T, preferred_element_type=jnp.float32)
    return (in_grad, grad_w_in, grad_w_out, grad_gain)

def reference(node_latent, agg_saved, node_cot, edge_latent, edge_cot, send_local, recv_local, send_slot, recv_slot, tile_count, edge_w_in, edge_w_out, edge_gain, node_w_in, node_w_out, node_gain):
    node_in = jnp.concatenate([node_latent, agg_saved], axis=1)
    node_cotangent = node_cot.astype(jnp.float32)
    node_in_grad, node_gw_in, node_gw_out, node_g_gain = mlp_backward(node_in, node_w_in, node_w_out, node_gain, node_cotangent)
    agg_grad = node_in_grad[:, H:].astype(jnp.bfloat16)
    tile_ids = jnp.arange(TILES * N_ROW, dtype=jnp.int32)
    owner = tile_ids // TILES
    sender_block = (owner + send_slot * STRIDE) % N_ROW
    receiver_block = (owner + recv_slot) % N_ROW
    senders = (sender_block[:, None] * NB + send_local).reshape(-1).astype(jnp.int32)
    receivers = (receiver_block[:, None] * NB + recv_local).reshape(-1).astype(jnp.int32)
    live_tiles = (tile_ids % TILES < tile_count[owner]).astype(jnp.float32)
    live_edges = jnp.repeat(live_tiles, TILE)[:, None]
    edge_in = jnp.concatenate([edge_latent, node_latent[senders], node_latent[receivers]], axis=1)
    edge_cotangent = live_edges * (edge_cot.astype(jnp.float32) + agg_grad[receivers].astype(jnp.float32))
    edge_in_grad, edge_gw_in, edge_gw_out, edge_g_gain = mlp_backward(edge_in, edge_w_in, edge_w_out, edge_gain, edge_cotangent)
    sender_grad = edge_in_grad[:, H:2 * H].astype(jnp.bfloat16)
    receiver_grad = edge_in_grad[:, 2 * H:].astype(jnp.bfloat16)
    node_total = node_cotangent + node_in_grad[:, :H] + jax.ops.segment_sum(sender_grad.astype(jnp.float32), senders, num_segments=NODES) + jax.ops.segment_sum(receiver_grad.astype(jnp.float32), receivers, num_segments=NODES)
    edge_total = edge_cotangent + edge_in_grad[:, :H]
    node_scale = NODES ** (-0.5)
    edge_scale = EDGES ** (-0.5)
    return (node_total.astype(jnp.bfloat16), edge_total.astype(jnp.bfloat16), edge_gw_in * edge_scale, edge_gw_out * edge_scale, edge_g_gain * edge_scale, node_gw_in * node_scale, node_gw_out * node_scale, node_g_gain * node_scale)
```

```python
import functools
import jax
import jax.numpy as jnp
from jax import lax
from jax.experimental import pallas as pl
from jax.experimental.pallas import tpu as pltpu
from jax.sharding import PartitionSpec as P

EPSILON = 1e-05
F32 = jnp.float32
BF16 = jnp.bfloat16
INNER = 4


def mm(a, b):
    return jnp.dot(a, b, preferred_element_type=F32)


def mm_nt(a, b):
    return lax.dot_general(a, b, (((1,), (1,)), ((), ())), preferred_element_type=F32)


def mm_tn(a, b):
    return lax.dot_general(a, b, (((0,), (0,)), ((), ())), preferred_element_type=F32)


def norm_backward(output, cotangent, gain):
    row_mean = jnp.mean(output, axis=-1, keepdims=True)
    centred = output - row_mean
    inverse = lax.rsqrt(jnp.mean(centred * centred, axis=-1, keepdims=True) + EPSILON)
    normed = centred * inverse
    grad_gain = jnp.sum(cotangent * normed, axis=0, keepdims=True)
    scaled = cotangent * gain
    out_grad = inverse * (
        scaled
        - jnp.mean(scaled, axis=-1, keepdims=True)
        - normed * jnp.mean(scaled * normed, axis=-1, keepdims=True)
    )
    return out_grad.astype(BF16), grad_gain


def pick(slot, options):
    return lax.select(slot == 0, options[0], lax.select(slot == 1, options[1], options[2]))


def layer_kernel(
    n,
    stride,
    fused,
    node_scale,
    edge_scale,
    x_ref,
    agg_ref,
    ncot_ref,
    e_ref,
    ecot_ref,
    sloc_ref,
    rloc_ref,
    sslot_ref,
    rslot_ref,
    count_ref,
    ewi_ref,
    ewo_ref,
    eg_ref,
    nwi_ref,
    nwo_ref,
    ng_ref,
    ngrad_ref,
    egrad_ref,
    egw_ref,
    ngw_ref,
    gains_ref,
    req,
    req_in,
    onehot,
    lat_out,
    lat_in,
    agg_out,
    agg_in,
    ret_out,
    ret_in,
    n_act,
    n_dout,
    n_dpre,
    n_agg,
    n_base,
    snd,
    rcv,
    e_pre,
    e_act,
    e_out,
    e_dout,
    e_dpre,
    gain_acc,
    w_src,
    w_a,
    w_sum,
    w_b_src,
    w_b,
    w_fin,
    g_a,
    g_b,
    send_sem,
    recv_sem,
):
    nb, h = x_ref.shape
    edges = e_ref.shape[0]
    tile = sloc_ref.shape[1]
    me = lax.axis_index("row")
    group = 4 * tile
    steps = [s for s in (1, 2)]
    hops = [0, stride, 2 * stride, 0, 1, 2]
    remote = (1, 2, 4, 5)
    outer = n // INNER
    ia, ib = lax.rem(me, INNER), me // INNER

    def at(offset):
        return lax.rem(me + offset % n, n)

    def inner_peer(i):
        return ib * INNER + lax.rem(ia + i, INNER)

    def outer_peer(i):
        return lax.rem(ib + i, outer) * INNER + ia

    partners = [at(o) for o in sorted({k for s in (1, 2) for d in (1, stride) for k in (s * d % n, -s * d % n)})]
    if fused:
        partners += [inner_peer(i) for i in range(1, INNER)]
        partners += [outer_peer(i) for i in range(1, outer)]
    barrier = pltpu.get_barrier_semaphore()
    for p in partners:
        pl.semaphore_signal(barrier, inc=1, device_id={"row": p}, device_id_type=pl.DeviceIdType.MESH)

    used = [0]

    def remote_copy(src, dst, target):
        k = used[0]
        used[0] += 1
        copy = pltpu.make_async_remote_copy(
            src_ref=src,
            dst_ref=dst,
            send_sem=send_sem.at[k],
            recv_sem=recv_sem.at[k],
            device_id={"row": target},
            device_id_type=pl.DeviceIdType.MESH,
        )
        copy.start()
        return copy

    for side, (loc, slot) in enumerate(((sloc_ref, sslot_ref), (rloc_ref, rslot_ref))):
        tiles = [loc[j : j + 1, :] for j in range(6)]
        none = jnp.full((1, tile), -1, jnp.int32)
        for s in range(3):
            k = side * 3 + s
            lead = lax.select(slot[0] == s, tiles[0], lax.select(slot[1] == s, tiles[1], tiles[2]))
            req[k, :, 0:tile] = lead
            for j in range(3):
                req[k, :, tile * (j + 1) : tile * (j + 2)] = lax.select(slot[3 + j] == s, tiles[3 + j], none)

    pl.semaphore_wait(barrier, len(partners))
    asks = {k: remote_copy(req.at[k], req_in.at[k], at(hops[k])) for k in remote}

    def make_onehot(k, index_ref):
        index = index_ref[k]

        def rows(i, carry):
            r = pl.multiple_of(i * 128, 128)
            ids = lax.broadcasted_iota(jnp.int32, (128, group), 0) + r
            onehot[k, pl.ds(r, 128), :] = (ids == index).astype(F32).astype(BF16)
            return carry

        lax.fori_loop(0, nb // 128, rows, 0)

    for k in (0, 3):
        make_onehot(k, req)
        lat_in[k] = mm_tn(onehot[k], x_ref[...]).astype(BF16)
    lats = {}
    for k in (2, 5, 1, 4):
        asks[k].wait()
        make_onehot(k, req_in)
        lat_out[k] = mm_tn(onehot[k], x_ref[...]).astype(BF16)
        lats[k] = remote_copy(lat_out.at[k], lat_in.at[k], at(-hops[k]))

    gain_acc[...] = jnp.zeros_like(gain_acc)

    def node_rows(i, carry):
        r = pl.ds(pl.multiple_of(i * 256, 256), 256)
        pre = mm(x_ref[r, :], nwi_ref[0:h, :]) + mm(agg_ref[r, :], nwi_ref[h:, :])
        sig = lax.logistic(pre)
        act = (pre * sig).astype(BF16)
        n_act[r, :] = act
        cot = ncot_ref[r, :].astype(F32)
        dout, gg = norm_backward(mm(act, nwo_ref[...]), cot, ng_ref[...])
        gain_acc[8:9, :] += gg
        n_dout[r, :] = dout
        dpre = (mm_nt(dout, nwo_ref[...]) * sig * (1.0 + pre * (1.0 - sig))).astype(BF16)
        n_dpre[r, :] = dpre
        n_agg[r, :] = mm_nt(dpre, nwi_ref[h:, :]).astype(BF16)
        n_base[r, :] = cot + mm_nt(dpre, nwi_ref[0:h, :])
        return carry

    lax.fori_loop(0, nb // 256, node_rows, 0)
    aggs = {}
    for s in (2, 1):
        agg_out[s] = mm_tn(onehot[3 + s], n_agg[...]).astype(BF16)
        aggs[s] = remote_copy(agg_out.at[s], agg_in.at[s], at(-s))
    agg_in[0] = mm_tn(onehot[3], n_agg[...]).astype(BF16)

    def rows_of(lo, rows, part):
        return pl.ds(pl.multiple_of(lo + part * rows, 16), rows)

    class Sum:
        def __init__(self, lo, total, scale, full):
            self.lo, self.total, self.scale, self.full = lo, total, scale, full
            self.q = total // INNER
            self.e = self.q // outer
            self.qlo, self.elo = lo // INNER, lo // INNER // outer

        def start_a(self):
            w_src[self.lo : self.lo + self.total, :] = self.full[...].astype(BF16)
            self.copies = [
                remote_copy(
                    w_src.at[rows_of(self.lo, self.q, lax.rem(ia + i, INNER)), :],
                    w_a.at[i - 1, pl.ds(self.qlo, self.q), :],
                    inner_peer(i),
                )
                for i in range(1, INNER)
            ]

        def start_b(self):
            for c in self.copies:
                c.wait()
            total = self.full[rows_of(0, self.q, ia), :]
            mine = pl.ds(self.qlo, self.q)
            for i in range(INNER - 1):
                total = total + w_a[i, mine, :].astype(F32)
            w_sum[mine, :] = total
            w_b_src[mine, :] = total.astype(BF16)
            self.copies = [
                remote_copy(
                    w_b_src.at[rows_of(self.qlo, self.e, lax.rem(ib + i, outer)), :],
                    w_b.at[i - 1, pl.ds(self.elo, self.e), :],
                    outer_peer(i),
                )
                for i in range(1, outer)
            ]

        def start_c(self):
            for c in self.copies:
                c.wait()
            total = w_sum[rows_of(self.qlo, self.e, ib), :]
            for i in range(outer - 1):
                total = total + w_b[i, pl.ds(self.elo, self.e), :].astype(F32)
            piece = pl.ds(pl.multiple_of(self.lo + ia * self.q + ib * self.e, 16), self.e)
            w_fin[piece, :] = (total * self.scale).astype(BF16)
            self.copies = [
                remote_copy(w_fin.at[piece, :], w_fin.at[piece, :], outer_peer(i)) for i in range(1, outer)
            ]

        def start_d(self):
            for c in self.copies:
                c.wait()
            piece = rows_of(self.lo, self.q, ia)
            self.copies = [
                remote_copy(w_fin.at[piece, :], w_fin.at[piece, :], inner_peer(i)) for i in range(1, INNER)
            ]

        def finish(self):
            for c in self.copies:
                c.wait()
            self.full[...] = w_fin[self.lo : self.lo + self.total, :].astype(F32)

    n_total = ngw_ref.shape[0]
    e_total = egw_ref.shape[0]
    edge_sum = Sum(0, e_total, edge_scale, egw_ref)
    node_sum = Sum(e_total, n_total, node_scale, ngw_ref)
    ngw_ref[0:h, :] = mm_tn(x_ref[...], n_dpre[...])
    ngw_ref[h : 2 * h, :] = mm_tn(agg_ref[...], n_dpre[...])
    ngw_ref[2 * h :, :] = mm_tn(n_act[...], n_dout[...])
    if fused:
        node_sum.start_a()

    def unpack(side, slot, buffer, table):
        for j in range(6):
            lo = 0 if j < 3 else tile * (j - 2)
            options = [buffer[side * 3 + s, lo : lo + tile, :] for s in range(3)]
            table[j * tile : (j + 1) * tile, :] = pick(slot[j], options)

    for k in (2, 1):
        lats[k].wait()
    unpack(0, sslot_ref, lat_in, snd)
    for k in (5, 4):
        lats[k].wait()
    unpack(1, rslot_ref, lat_in, rcv)
    if fused:
        node_sum.start_b()

    def edge_forward(i, carry):
        r = pl.ds(pl.multiple_of(i * 256, 256), 256)
        pre = mm(e_ref[r, :], ewi_ref[0:h, :]) + mm(snd[r, :], ewi_ref[h : 2 * h, :]) + mm(rcv[r, :], ewi_ref[2 * h :, :])
        e_pre[r, :] = pre
        act = (pre * lax.logistic(pre)).astype(BF16)
        e_act[r, :] = act
        e_out[r, :] = mm(act, ewo_ref[...])
        return carry

    lax.fori_loop(0, edges // 256, edge_forward, 0)
    if fused:
        node_sum.start_c()
    for s in (2, 1):
        aggs[s].wait()
    unpack(0, rslot_ref, agg_in, e_dpre)
    live_rows = count_ref[0] * tile

    def edge_backward(i, carry):
        lo = pl.multiple_of(i * 256, 256)
        r = pl.ds(lo, 256)
        live = (lax.broadcasted_iota(jnp.int32, (256, h), 0) + lo) < live_rows
        cot = jnp.where(live, ecot_ref[r, :].astype(F32) + e_dpre[r, :].astype(F32), 0.0)
        dout, gg = norm_backward(e_out[r, :], cot, eg_ref[...])
        gain_acc[0:1, :] += gg
        e_dout[r, :] = dout
        pre = e_pre[r, :]
        sig = lax.logistic(pre)
        dpre = (mm_nt(dout, ewo_ref[...]) * sig * (1.0 + pre * (1.0 - sig))).astype(BF16)
        e_dpre[r, :] = dpre
        egrad_ref[r, :] = (cot + mm_nt(dpre, ewi_ref[0:h, :])).astype(BF16)
        e_out[r, :] = mm_nt(dpre, ewi_ref[h : 2 * h, :])
        e_pre[r, :] = mm_nt(dpre, ewi_ref[2 * h :, :])
        return carry

    lax.fori_loop(0, edges // 256, edge_backward, 0)

    rets = {}
    for k in (2, 5, 1, 4, 0, 3):
        s = k % 3
        grads, slot = (e_out, sslot_ref) if k < 3 else (e_pre, rslot_ref)
        target = ret_in if s == 0 else ret_out
        lead = [grads[j * tile : (j + 1) * tile, :] for j in range(3)]
        lead = lax.select(slot[0] == s, lead[0], lax.select(slot[1] == s, lead[1], lead[2]))
        target[k, 0:tile, :] = lead.astype(BF16)
        target[k, tile:, :] = grads[3 * tile :, :].astype(BF16)
        if s:
            rets[k] = remote_copy(ret_out.at[k], ret_in.at[k], at(hops[k]))

    if fused:
        node_sum.start_d()
    egw_ref[0:h, :] = mm_tn(e_ref[...], e_dpre[...])
    egw_ref[h : 2 * h, :] = mm_tn(snd[...], e_dpre[...])
    egw_ref[2 * h : 3 * h, :] = mm_tn(rcv[...], e_dpre[...])
    egw_ref[3 * h :, :] = mm_tn(e_act[...], e_dout[...])
    if fused:
        edge_sum.start_a()
        g_a[ia] = gain_acc[...]
        gains = [remote_copy(gain_acc, g_a.at[ia], inner_peer(i)) for i in range(1, INNER)]

    n_base[...] += mm(onehot[0], ret_in[0]) + mm(onehot[3], ret_in[3])
    if fused:
        node_sum.finish()
        edge_sum.start_b()
        for c in gains:
            c.wait()
        g_sum = g_a[0]
        for i in range(1, INNER):
            g_sum = g_sum + g_a[i]
        gain_acc[...] = g_sum
        g_b[ib] = g_sum
        gains = [remote_copy(gain_acc, g_b.at[ib], outer_peer(i)) for i in range(1, outer)]
        edge_sum.start_c()
    for k in (1, 4):
        rets[k].wait()
    n_base[...] += mm(onehot[1], ret_in[1]) + mm(onehot[4], ret_in[4])
    if fused:
        edge_sum.start_d()
    for k in (2, 5):
        rets[k].wait()
    total = n_base[...] + mm(onehot[2], ret_in[2]) + mm(onehot[5], ret_in[5])
    ngrad_ref[...] = total.astype(BF16)
    if fused:
        for c in gains:
            c.wait()
        g_sum = g_b[0]
        for i in range(1, outer):
            g_sum = g_sum + g_b[i]
        gains_ref[0:8, :] = g_sum[0:8, :] * edge_scale
        gains_ref[8:16, :] = g_sum[8:16, :] * node_scale
        edge_sum.finish()
    else:
        gains_ref[...] = gain_acc[...]


def on_device(
    node_latent,
    agg_saved,
    node_cot,
    edge_latent,
    edge_cot,
    send_local,
    recv_local,
    send_slot,
    recv_slot,
    tile_count,
    edge_w_in,
    edge_w_out,
    edge_gain,
    node_w_in,
    node_w_out,
    node_gain,
):
    nb, h = node_latent.shape
    edges = edge_latent.shape[0]
    tile_total, tile = send_local.shape
    n = lax.axis_size("row")
    stride = n // 8
    node_scale = (nb * n) ** (-0.5)
    edge_scale = (edges * n) ** (-0.5)
    outer = n // INNER
    fused = n % INNER == 0 and 3 * h % (INNER * outer * 16) == 0 and 4 * h % (INNER * outer * 16) == 0
    levels = outer if fused else 2
    group = 4 * tile
    weights = 7 * h
    vmem = pl.BlockSpec(memory_space=pltpu.VMEM)
    smem = pl.BlockSpec(memory_space=pltpu.SMEM)
    copies = 14 + (2 * (2 * (INNER - 1) + 2 * (outer - 1)) + INNER - 1 + outer - 1 if fused else 0)
    node_grad, edge_grad, egw, ngw, gains = pl.pallas_call(
        functools.partial(layer_kernel, n, stride, fused, node_scale, edge_scale),
        out_shape=(
            jax.ShapeDtypeStruct((nb, h), BF16),
            jax.ShapeDtypeStruct((edges, h), BF16),
            jax.ShapeDtypeStruct((4 * h, h), F32),
            jax.ShapeDtypeStruct((3 * h, h), F32),
            jax.ShapeDtypeStruct((16, h), F32),
        ),
        in_specs=[vmem] * 7 + [smem] * 3 + [vmem] * 6,
        out_specs=(vmem,) * 5,
        scratch_shapes=[
            pltpu.VMEM((6, 1, group), jnp.int32),
            pltpu.VMEM((6, 1, group), jnp.int32),
            pltpu.VMEM((6, nb, group), BF16),
            pltpu.VMEM((6, group, h), BF16),
            pltpu.VMEM((6, group, h), BF16),
            pltpu.VMEM((3, group, h), BF16),
            pltpu.VMEM((3, group, h), BF16),
            pltpu.VMEM((6, group, h), BF16),
            pltpu.VMEM((6, group, h), BF16),
            pltpu.VMEM((nb, h), BF16),
            pltpu.VMEM((nb, h), BF16),
            pltpu.VMEM((nb, h), BF16),
            pltpu.VMEM((nb, h), BF16),
            pltpu.VMEM((nb, h), F32),
            pltpu.VMEM((edges, h), BF16),
            pltpu.VMEM((edges, h), BF16),
            pltpu.VMEM((edges, h), F32),
            pltpu.VMEM((edges, h), BF16),
            pltpu.VMEM((edges, h), F32),
            pltpu.VMEM((edges, h), BF16),
            pltpu.VMEM((edges, h), BF16),
            pltpu.VMEM((16, h), F32),
            pltpu.VMEM((weights, h), BF16),
            pltpu.VMEM((INNER - 1, weights // INNER, h), BF16),
            pltpu.VMEM((weights // INNER, h), F32),
            pltpu.VMEM((weights // INNER, h), BF16),
            pltpu.VMEM((levels - 1, weights // INNER // levels, h), BF16),
            pltpu.VMEM((weights, h), BF16),
            pltpu.VMEM((INNER, 16, h), F32),
            pltpu.VMEM((levels, 16, h), F32),
            pltpu.SemaphoreType.DMA((copies,)),
            pltpu.SemaphoreType.DMA((copies,)),
        ],
        compiler_params=pltpu.CompilerParams(
            collective_id=0, has_side_effects=True, vmem_limit_bytes=50 * 1024 * 1024
        ),
        cost_estimate=pl.CostEstimate(flops=7 * 10**9, bytes_accessed=8 * 10**6, transcendentals=10**6),
    )(
        node_latent,
        agg_saved,
        node_cot,
        edge_latent,
        edge_cot,
        send_local,
        recv_local,
        send_slot,
        recv_slot,
        tile_count,
        edge_w_in,
        edge_w_out,
        edge_gain[None, :],
        node_w_in,
        node_w_out,
        node_gain[None, :],
    )
    if not fused:
        egw, ngw, gains = lax.psum((egw * edge_scale, ngw * node_scale, gains), "row")
        gains = gains * jnp.repeat(jnp.array([edge_scale, node_scale], F32), 8)[:, None]
    return (
        node_grad,
        edge_grad,
        egw[: 3 * h],
        egw[3 * h :],
        gains[0],
        ngw[: 2 * h],
        ngw[2 * h :],
        gains[8],
    )


def solution(mesh):
    placed = (P(("parts", "row"), None),) * 7 + (P(("parts", "row")),) * 3 + (P(),) * 6
    return jax.shard_map(
        on_device,
        mesh=mesh,
        in_specs=placed,
        out_specs=(
            P(("parts", "row"), None),
            P(("parts", "row"), None),
            P("parts", None),
            P("parts", None),
            P("parts"),
            P("parts", None),
            P("parts", None),
            P("parts"),
        ),
        check_vma=False,
    )
```

```python
import functools
import jax
import jax.numpy as jnp
from jax import lax
from jax.experimental import pallas as pl
from jax.experimental.pallas import tpu as pltpu
from jax.sharding import PartitionSpec as P

EPSILON = 1e-05
F32 = jnp.float32
BF16 = jnp.bfloat16
INNER = 4


def mm(a, b):
    return jnp.dot(a, b, preferred_element_type=F32)


def mm_nt(a, b):
    return lax.dot_general(a, b, (((1,), (1,)), ((), ())), preferred_element_type=F32)


def mm_tn(a, b):
    return lax.dot_general(a, b, (((0,), (0,)), ((), ())), preferred_element_type=F32)


def norm_backward(output, cotangent, gain):
    row_mean = jnp.mean(output, axis=-1, keepdims=True)
    centred = output - row_mean
    inverse = lax.rsqrt(jnp.mean(centred * centred, axis=-1, keepdims=True) + EPSILON)
    normed = centred * inverse
    grad_gain = jnp.sum(cotangent * normed, axis=0, keepdims=True)
    scaled = cotangent * gain
    out_grad = inverse * (
        scaled
        - jnp.mean(scaled, axis=-1, keepdims=True)
        - normed * jnp.mean(scaled * normed, axis=-1, keepdims=True)
    )
    return out_grad.astype(BF16), grad_gain


def pick(slot, options):
    return lax.select(slot == 0, options[0], lax.select(slot == 1, options[1], options[2]))


def layer_kernel(
    n,
    stride,
    fused,
    node_scale,
    edge_scale,
    x_hbm,
    agg_hbm,
    ncot_hbm,
    e_hbm,
    ecot_hbm,
    sloc_hbm,
    rloc_hbm,
    sslot_ref,
    rslot_ref,
    count_ref,
    ewi_hbm,
    ewo_hbm,
    eg_hbm,
    nwi_hbm,
    nwo_hbm,
    ng_hbm,
    ngrad_ref,
    egrad_ref,
    egwi_out,
    egwo_out,
    ngwi_out,
    ngwo_out,
    egain_out,
    ngain_out,
    x_ref,
    agg_ref,
    ncot_ref,
    e_ref,
    ecot_ref,
    sloc_ref,
    rloc_ref,
    ewi_ref,
    ewo_ref,
    eg_ref,
    nwi_ref,
    nwo_ref,
    ng_ref,
    egw_ref,
    ngw_ref,
    load_sem,
    req,
    req_in,
    onehot,
    lat_out,
    lat_in,
    agg_out,
    agg_in,
    ret_out,
    ret_in,
    n_act,
    n_dout,
    n_dpre,
    n_agg,
    n_base,
    snd,
    rcv,
    e_pre,
    e_act,
    e_out,
    e_dout,
    e_dpre,
    gain_acc,
    w_src,
    w_a,
    w_sum,
    w_b_src,
    w_b,
    w_fin,
    g_a,
    g_b,
    send_sem,
    recv_sem,
):
    nb, h = x_ref.shape
    edges = e_ref.shape[0]
    loads = {}
    for i, (name, src, dst) in enumerate(
        (
            ("sloc", sloc_hbm, sloc_ref),
            ("rloc", rloc_hbm, rloc_ref),
            ("x", x_hbm, x_ref),
            ("nwi", nwi_hbm, nwi_ref),
            ("agg", agg_hbm, agg_ref),
            ("nwo", nwo_hbm, nwo_ref),
            ("ng", ng_hbm, ng_ref),
            ("ncot", ncot_hbm, ncot_ref),
            ("e", e_hbm, e_ref),
            ("ewi", ewi_hbm, ewi_ref),
            ("ewo", ewo_hbm, ewo_ref),
            ("eg", eg_hbm, eg_ref),
            ("ecot", ecot_hbm, ecot_ref),
        )
    ):
        loads[name] = pltpu.make_async_copy(src, dst, load_sem.at[i])
    tile = sloc_ref.shape[1]
    me = lax.axis_index("row")
    group = 4 * tile
    steps = [s for s in (1, 2)]
    hops = [0, stride, 2 * stride, 0, 1, 2]
    remote = (1, 2, 4, 5)
    outer = n // INNER
    ia, ib = lax.rem(me, INNER), me // INNER

    def at(offset):
        return lax.rem(me + offset % n, n)

    def inner_peer(i):
        return ib * INNER + lax.rem(ia + i, INNER)

    def outer_peer(i):
        return lax.rem(ib + i, outer) * INNER + ia

    partners = [at(o) for o in sorted({k for s in (1, 2) for d in (1, stride) for k in (s * d % n, -s * d % n)})]
    if fused:
        partners += [inner_peer(i) for i in range(1, INNER)]
        partners += [outer_peer(i) for i in range(1, outer)]
    barrier = pltpu.get_barrier_semaphore()
    for p in partners:
        pl.semaphore_signal(barrier, inc=1, device_id={"row": p}, device_id_type=pl.DeviceIdType.MESH)

    for c in loads.values():
        c.start()

    used = [0]

    def remote_copy(src, dst, target):
        k = used[0]
        used[0] += 1
        copy = pltpu.make_async_remote_copy(
            src_ref=src,
            dst_ref=dst,
            send_sem=send_sem.at[k],
            recv_sem=recv_sem.at[k],
            device_id={"row": target},
            device_id_type=pl.DeviceIdType.MESH,
        )
        copy.start()
        return copy

    loads["sloc"].wait()
    loads["rloc"].wait()
    for side, (loc, slot) in enumerate(((sloc_ref, sslot_ref), (rloc_ref, rslot_ref))):
        tiles = [loc[j : j + 1, :] for j in range(6)]
        none = jnp.full((1, tile), -1, jnp.int32)
        for s in range(3):
            k = side * 3 + s
            lead = lax.select(slot[0] == s, tiles[0], lax.select(slot[1] == s, tiles[1], tiles[2]))
            req[k, :, 0:tile] = lead
            for j in range(3):
                req[k, :, tile * (j + 1) : tile * (j + 2)] = lax.select(slot[3 + j] == s, tiles[3 + j], none)

    pl.semaphore_wait(barrier, len(partners))
    asks = {k: remote_copy(req.at[k], req_in.at[k], at(hops[k])) for k in remote}

    def make_onehot(k, index_ref):
        index = index_ref[k]

        def rows(i, carry):
            r = pl.multiple_of(i * 128, 128)
            ids = lax.broadcasted_iota(jnp.int32, (128, group), 0) + r
            onehot[k, pl.ds(r, 128), :] = (ids == index).astype(F32).astype(BF16)
            return carry

        lax.fori_loop(0, nb // 128, rows, 0)

    loads["x"].wait()
    for k in (0, 3):
        make_onehot(k, req)
        lat_in[k] = mm_tn(onehot[k], x_ref[...]).astype(BF16)
    lats = {}
    for k in (2, 5, 1, 4):
        asks[k].wait()
        make_onehot(k, req_in)
        lat_out[k] = mm_tn(onehot[k], x_ref[...]).astype(BF16)
        lats[k] = remote_copy(lat_out.at[k], lat_in.at[k], at(-hops[k]))

    gain_acc[...] = jnp.zeros_like(gain_acc)
    for name in ("nwi", "agg", "nwo", "ng", "ncot"):
        loads[name].wait()

    def node_rows(i, carry):
        r = pl.ds(pl.multiple_of(i * 256, 256), 256)
        pre = mm(x_ref[r, :], nwi_ref[0:h, :]) + mm(agg_ref[r, :], nwi_ref[h:, :])
        sig = lax.logistic(pre)
        act = (pre * sig).astype(BF16)
        n_act[r, :] = act
        cot = ncot_ref[r, :].astype(F32)
        dout, gg = norm_backward(mm(act, nwo_ref[...]), cot, ng_ref[...])
        gain_acc[8:9, :] += gg
        n_dout[r, :] = dout
        dpre = (mm_nt(dout, nwo_ref[...]) * sig * (1.0 + pre * (1.0 - sig))).astype(BF16)
        n_dpre[r, :] = dpre
        n_agg[r, :] = mm_nt(dpre, nwi_ref[h:, :]).astype(BF16)
        n_base[r, :] = cot + mm_nt(dpre, nwi_ref[0:h, :])
        return carry

    lax.fori_loop(0, nb // 256, node_rows, 0)
    aggs = {}
    for s in (2, 1):
        agg_out[s] = mm_tn(onehot[3 + s], n_agg[...]).astype(BF16)
        aggs[s] = remote_copy(agg_out.at[s], agg_in.at[s], at(-s))
    agg_in[0] = mm_tn(onehot[3], n_agg[...]).astype(BF16)

    def rows_of(lo, rows, part):
        return pl.ds(pl.multiple_of(lo + part * rows, 16), rows)

    def give_weights(outs, rows):
        split = outs[0].shape[0]
        outs[0][...] = rows(0, split)
        outs[1][...] = rows(split, split + h)

    class Sum:
        def __init__(self, lo, total, scale, full, outs):
            self.outs = outs
            self.lo, self.total, self.scale, self.full = lo, total, scale, full
            self.q = total // INNER
            self.e = self.q // outer
            self.qlo, self.elo = lo // INNER, lo // INNER // outer

        def start_a(self):
            w_src[self.lo : self.lo + self.total, :] = self.full[...].astype(BF16)
            self.copies = [
                remote_copy(
                    w_src.at[rows_of(self.lo, self.q, lax.rem(ia + i, INNER)), :],
                    w_a.at[i - 1, pl.ds(self.qlo, self.q), :],
                    inner_peer(i),
                )
                for i in range(1, INNER)
            ]

        def start_b(self):
            for c in self.copies:
                c.wait()
            total = self.full[rows_of(0, self.q, ia), :]
            mine = pl.ds(self.qlo, self.q)
            for i in range(INNER - 1):
                total = total + w_a[i, mine, :].astype(F32)
            w_sum[mine, :] = total
            w_b_src[mine, :] = total.astype(BF16)
            self.copies = [
                remote_copy(
                    w_b_src.at[rows_of(self.qlo, self.e, lax.rem(ib + i, outer)), :],
                    w_b.at[i - 1, pl.ds(self.elo, self.e), :],
                    outer_peer(i),
                )
                for i in range(1, outer)
            ]

        def start_c(self):
            for c in self.copies:
                c.wait()
            total = w_sum[rows_of(self.qlo, self.e, ib), :]
            for i in range(outer - 1):
                total = total + w_b[i, pl.ds(self.elo, self.e), :].astype(F32)
            piece = pl.ds(pl.multiple_of(self.lo + ia * self.q + ib * self.e, 16), self.e)
            w_fin[piece, :] = (total * self.scale).astype(BF16)
            self.copies = [
                remote_copy(w_fin.at[piece, :], w_fin.at[piece, :], outer_peer(i)) for i in range(1, outer)
            ]

        def start_d(self):
            for c in self.copies:
                c.wait()
            piece = rows_of(self.lo, self.q, ia)
            self.copies = [
                remote_copy(w_fin.at[piece, :], w_fin.at[piece, :], inner_peer(i)) for i in range(1, INNER)
            ]

        def finish(self):
            for c in self.copies:
                c.wait()
            give_weights(self.outs, lambda a, b: w_fin[self.lo + a : self.lo + b, :])

    n_total = ngw_ref.shape[0]
    e_total = egw_ref.shape[0]
    edge_sum = Sum(0, e_total, edge_scale, egw_ref, (egwi_out, egwo_out))
    node_sum = Sum(e_total, n_total, node_scale, ngw_ref, (ngwi_out, ngwo_out))
    ngw_ref[0:h, :] = mm_tn(x_ref[...], n_dpre[...])
    ngw_ref[h : 2 * h, :] = mm_tn(agg_ref[...], n_dpre[...])
    ngw_ref[2 * h :, :] = mm_tn(n_act[...], n_dout[...])
    if fused:
        node_sum.start_a()

    for name in ("e", "ewi", "ewo", "eg", "ecot"):
        loads[name].wait()
    def unpack(side, slot, buffer, table):
        for j in range(6):
            lo = 0 if j < 3 else tile * (j - 2)
            options = [buffer[side * 3 + s, lo : lo + tile, :] for s in range(3)]
            table[j * tile : (j + 1) * tile, :] = pick(slot[j], options)

    for k in (2, 1):
        lats[k].wait()
    unpack(0, sslot_ref, lat_in, snd)
    for k in (5, 4):
        lats[k].wait()
    unpack(1, rslot_ref, lat_in, rcv)
    if fused:
        node_sum.start_b()

    def edge_forward(i, carry):
        r = pl.ds(pl.multiple_of(i * 256, 256), 256)
        pre = mm(e_ref[r, :], ewi_ref[0:h, :]) + mm(snd[r, :], ewi_ref[h : 2 * h, :]) + mm(rcv[r, :], ewi_ref[2 * h :, :])
        e_pre[r, :] = pre
        act = (pre * lax.logistic(pre)).astype(BF16)
        e_act[r, :] = act
        e_out[r, :] = mm(act, ewo_ref[...])
        return carry

    lax.fori_loop(0, edges // 256, edge_forward, 0)
    if fused:
        node_sum.start_c()
    for s in (2, 1):
        aggs[s].wait()
    unpack(0, rslot_ref, agg_in, e_dpre)
    live_rows = count_ref[0] * tile

    def edge_backward(i, carry):
        lo = pl.multiple_of(i * 256, 256)
        r = pl.ds(lo, 256)
        live = (lax.broadcasted_iota(jnp.int32, (256, h), 0) + lo) < live_rows
        cot = jnp.where(live, ecot_ref[r, :].astype(F32) + e_dpre[r, :].astype(F32), 0.0)
        dout, gg = norm_backward(e_out[r, :], cot, eg_ref[...])
        gain_acc[0:1, :] += gg
        e_dout[r, :] = dout
        pre = e_pre[r, :]
        sig = lax.logistic(pre)
        dpre = (mm_nt(dout, ewo_ref[...]) * sig * (1.0 + pre * (1.0 - sig))).astype(BF16)
        e_dpre[r, :] = dpre
        egrad_ref[r, :] = (cot + mm_nt(dpre, ewi_ref[0:h, :])).astype(BF16)
        e_out[r, :] = mm_nt(dpre, ewi_ref[h : 2 * h, :])
        e_pre[r, :] = mm_nt(dpre, ewi_ref[2 * h :, :])
        return carry

    lax.fori_loop(0, edges // 256, edge_backward, 0)

    rets = {}
    for k in (2, 5, 1, 4, 0, 3):
        s = k % 3
        grads, slot = (e_out, sslot_ref) if k < 3 else (e_pre, rslot_ref)
        target = ret_in if s == 0 else ret_out
        lead = [grads[j * tile : (j + 1) * tile, :] for j in range(3)]
        lead = lax.select(slot[0] == s, lead[0], lax.select(slot[1] == s, lead[1], lead[2]))
        target[k, 0:tile, :] = lead.astype(BF16)
        target[k, tile:, :] = grads[3 * tile :, :].astype(BF16)
        if s:
            rets[k] = remote_copy(ret_out.at[k], ret_in.at[k], at(hops[k]))

    if fused:
        node_sum.start_d()
    egw_ref[0:h, :] = mm_tn(e_ref[...], e_dpre[...])
    egw_ref[h : 2 * h, :] = mm_tn(snd[...], e_dpre[...])
    egw_ref[2 * h : 3 * h, :] = mm_tn(rcv[...], e_dpre[...])
    egw_ref[3 * h :, :] = mm_tn(e_act[...], e_dout[...])
    if fused:
        edge_sum.start_a()
        g_a[ia] = gain_acc[...]
        gains = [remote_copy(gain_acc, g_a.at[ia], inner_peer(i)) for i in range(1, INNER)]

    n_base[...] += mm(onehot[0], ret_in[0]) + mm(onehot[3], ret_in[3])
    if fused:
        node_sum.finish()
        edge_sum.start_b()
        for c in gains:
            c.wait()
        g_sum = g_a[0]
        for i in range(1, INNER):
            g_sum = g_sum + g_a[i]
        gain_acc[...] = g_sum
        g_b[ib] = g_sum
        gains = [remote_copy(gain_acc, g_b.at[ib], outer_peer(i)) for i in range(1, outer)]
        edge_sum.start_c()
    for k in (1, 4):
        rets[k].wait()
    n_base[...] += mm(onehot[1], ret_in[1]) + mm(onehot[4], ret_in[4])
    if fused:
        edge_sum.start_d()
    for k in (2, 5):
        rets[k].wait()
    total = n_base[...] + mm(onehot[2], ret_in[2]) + mm(onehot[5], ret_in[5])
    ngrad_ref[...] = total.astype(BF16)
    if fused:
        for c in gains:
            c.wait()
        g_sum = g_b[0]
        for i in range(1, outer):
            g_sum = g_sum + g_b[i]
        egain_out[...] = g_sum[0:1, :] * edge_scale
        ngain_out[...] = g_sum[8:9, :] * node_scale
        edge_sum.finish()
    else:
        egain_out[...] = gain_acc[0:1, :] * edge_scale
        ngain_out[...] = gain_acc[8:9, :] * node_scale
        give_weights(edge_sum.outs, lambda a, b: egw_ref[a:b, :] * edge_scale)
        give_weights(node_sum.outs, lambda a, b: ngw_ref[a:b, :] * node_scale)


def on_device(
    node_latent,
    agg_saved,
    node_cot,
    edge_latent,
    edge_cot,
    send_local,
    recv_local,
    send_slot,
    recv_slot,
    tile_count,
    edge_w_in,
    edge_w_out,
    edge_gain,
    node_w_in,
    node_w_out,
    node_gain,
):
    nb, h = node_latent.shape
    edges = edge_latent.shape[0]
    tile_total, tile = send_local.shape
    n = lax.axis_size("row")
    stride = n // 8
    node_scale = (nb * n) ** (-0.5)
    edge_scale = (edges * n) ** (-0.5)
    outer = n // INNER
    fused = n % INNER == 0 and 3 * h % (INNER * outer * 16) == 0 and 4 * h % (INNER * outer * 16) == 0
    levels = outer if fused else 2
    group = 4 * tile
    weights = 7 * h
    vmem = pl.BlockSpec(memory_space=pltpu.VMEM)
    smem = pl.BlockSpec(memory_space=pltpu.SMEM)
    copies = 14 + (2 * (2 * (INNER - 1) + 2 * (outer - 1)) + INNER - 1 + outer - 1 if fused else 0)
    anywhere = pl.BlockSpec(memory_space=pl.ANY)
    summed = BF16 if fused else F32
    node_grad, edge_grad, *sums = pl.pallas_call(
        functools.partial(layer_kernel, n, stride, fused, node_scale, edge_scale),
        out_shape=(
            jax.ShapeDtypeStruct((nb, h), BF16),
            jax.ShapeDtypeStruct((edges, h), BF16),
            jax.ShapeDtypeStruct((3 * h, h), summed),
            jax.ShapeDtypeStruct((h, h), summed),
            jax.ShapeDtypeStruct((2 * h, h), summed),
            jax.ShapeDtypeStruct((h, h), summed),
            jax.ShapeDtypeStruct((1, h), F32),
            jax.ShapeDtypeStruct((1, h), F32),
        ),
        in_specs=[anywhere] * 7 + [smem] * 3 + [anywhere] * 6,
        out_specs=(vmem,) * 8,
        scratch_shapes=[
            pltpu.VMEM((nb, h), BF16),
            pltpu.VMEM((nb, h), BF16),
            pltpu.VMEM((nb, h), BF16),
            pltpu.VMEM((edges, h), BF16),
            pltpu.VMEM((edges, h), BF16),
            pltpu.VMEM((tile_total, tile), jnp.int32),
            pltpu.VMEM((tile_total, tile), jnp.int32),
            pltpu.VMEM((3 * h, h), BF16),
            pltpu.VMEM((h, h), BF16),
            pltpu.VMEM((1, h), F32),
            pltpu.VMEM((2 * h, h), BF16),
            pltpu.VMEM((h, h), BF16),
            pltpu.VMEM((1, h), F32),
            pltpu.VMEM((4 * h, h), F32),
            pltpu.VMEM((3 * h, h), F32),
            pltpu.SemaphoreType.DMA((13,)),
            pltpu.VMEM((6, 1, group), jnp.int32),
            pltpu.VMEM((6, 1, group), jnp.int32),
            pltpu.VMEM((6, nb, group), BF16),
            pltpu.VMEM((6, group, h), BF16),
            pltpu.VMEM((6, group, h), BF16),
            pltpu.VMEM((3, group, h), BF16),
            pltpu.VMEM((3, group, h), BF16),
            pltpu.VMEM((6, group, h), BF16),
            pltpu.VMEM((6, group, h), BF16),
            pltpu.VMEM((nb, h), BF16),
            pltpu.VMEM((nb, h), BF16),
            pltpu.VMEM((nb, h), BF16),
            pltpu.VMEM((nb, h), BF16),
            pltpu.VMEM((nb, h), F32),
            pltpu.VMEM((edges, h), BF16),
            pltpu.VMEM((edges, h), BF16),
            pltpu.VMEM((edges, h), F32),
            pltpu.VMEM((edges, h), BF16),
            pltpu.VMEM((edges, h), F32),
            pltpu.VMEM((edges, h), BF16),
            pltpu.VMEM((edges, h), BF16),
            pltpu.VMEM((16, h), F32),
            pltpu.VMEM((weights, h), BF16),
            pltpu.VMEM((INNER - 1, weights // INNER, h), BF16),
            pltpu.VMEM((weights // INNER, h), F32),
            pltpu.VMEM((weights // INNER, h), BF16),
            pltpu.VMEM((levels - 1, weights // INNER // levels, h), BF16),
            pltpu.VMEM((weights, h), BF16),
            pltpu.VMEM((INNER, 16, h), F32),
            pltpu.VMEM((levels, 16, h), F32),
            pltpu.SemaphoreType.DMA((copies,)),
            pltpu.SemaphoreType.DMA((copies,)),
        ],
        compiler_params=pltpu.CompilerParams(
            collective_id=0, has_side_effects=True, vmem_limit_bytes=60 * 1024 * 1024
        ),
        cost_estimate=pl.CostEstimate(flops=7 * 10**9, bytes_accessed=8 * 10**6, transcendentals=10**6),
    )(
        node_latent,
        agg_saved,
        node_cot,
        edge_latent,
        edge_cot,
        send_local,
        recv_local,
        send_slot,
        recv_slot,
        tile_count,
        edge_w_in,
        edge_w_out,
        edge_gain[None, :],
        node_w_in,
        node_w_out,
        node_gain[None, :],
    )
    if not fused:
        sums = lax.psum(tuple(sums), "row")
    egwi, egwo, ngwi, ngwo, egain, ngain = [v.astype(F32) for v in sums]
    return (node_grad, edge_grad, egwi, egwo, egain[0], ngwi, ngwo, ngain[0])


def solution(mesh):
    placed = (P(("parts", "row"), None),) * 7 + (P(("parts", "row")),) * 3 + (P(),) * 6
    return jax.shard_map(
        on_device,
        mesh=mesh,
        in_specs=placed,
        out_specs=(
            P(("parts", "row"), None),
            P(("parts", "row"), None),
            P("parts", None),
            P("parts", None),
            P("parts"),
            P("parts", None),
            P("parts", None),
            P("parts"),
        ),
        check_vma=False,
    )
```

```python
import functools
import jax
import jax.numpy as jnp
from jax import lax
from jax.experimental import pallas as pl
from jax.experimental.pallas import tpu as pltpu
from jax.sharding import PartitionSpec as P

EPSILON = 1e-05
F32 = jnp.float32
BF16 = jnp.bfloat16
INNER = 4


def mm(a, b):
    return jnp.dot(a, b, preferred_element_type=F32)


def mm_nt(a, b):
    return lax.dot_general(a, b, (((1,), (1,)), ((), ())), preferred_element_type=F32)


def mm_tn(a, b):
    return lax.dot_general(a, b, (((0,), (0,)), ((), ())), preferred_element_type=F32)


def norm_backward(output, cotangent, gain):
    row_mean = jnp.mean(output, axis=-1, keepdims=True)
    centred = output - row_mean
    inverse = lax.rsqrt(jnp.mean(centred * centred, axis=-1, keepdims=True) + EPSILON)
    normed = centred * inverse
    grad_gain = jnp.sum(cotangent * normed, axis=0, keepdims=True)
    scaled = cotangent * gain
    out_grad = inverse * (
        scaled
        - jnp.mean(scaled, axis=-1, keepdims=True)
        - normed * jnp.mean(scaled * normed, axis=-1, keepdims=True)
    )
    return out_grad.astype(BF16), grad_gain


def pick(slot, options):
    return lax.select(slot == 0, options[0], lax.select(slot == 1, options[1], options[2]))


def layer_kernel(
    n,
    stride,
    fused,
    node_scale,
    edge_scale,
    x_hbm,
    agg_hbm,
    ncot_hbm,
    e_hbm,
    ecot_hbm,
    sloc_hbm,
    rloc_hbm,
    sslot_ref,
    rslot_ref,
    count_ref,
    ewi_hbm,
    ewo_hbm,
    eg_hbm,
    nwi_hbm,
    nwo_hbm,
    ng_hbm,
    ngrad_ref,
    egrad_ref,
    egwi_out,
    egwo_out,
    ngwi_out,
    ngwo_out,
    egain_out,
    ngain_out,
    x_ref,
    agg_ref,
    ncot_ref,
    e_ref,
    ecot_ref,
    sloc_ref,
    rloc_ref,
    ewi_ref,
    ewo_ref,
    eg_ref,
    nwi_ref,
    nwo_ref,
    ng_ref,
    egw_ref,
    ngw_ref,
    load_sem,
    req,
    req_in,
    onehot,
    lat_out,
    lat_in,
    agg_out,
    agg_in,
    ret_out,
    ret_in,
    n_act,
    n_dout,
    n_dpre,
    n_agg,
    n_base,
    snd,
    rcv,
    e_pre,
    e_act,
    e_out,
    e_dout,
    e_dpre,
    gain_acc,
    w_src,
    w_a,
    w_sum,
    w_b_src,
    w_b,
    w_fin,
    g_a,
    g_b,
    hold,
    send_sem,
    recv_sem,
):
    nb, h = x_ref.shape
    edges = e_ref.shape[0]
    loads = {}
    for i, (name, src, dst) in enumerate(
        (
            ("sloc", sloc_hbm, sloc_ref),
            ("rloc", rloc_hbm, rloc_ref),
            ("x", x_hbm, x_ref),
            ("nwi", nwi_hbm, nwi_ref),
            ("agg", agg_hbm, agg_ref),
            ("nwo", nwo_hbm, nwo_ref),
            ("ng", ng_hbm, ng_ref),
            ("ncot", ncot_hbm, ncot_ref),
            ("e", e_hbm, e_ref),
            ("ewi", ewi_hbm, ewi_ref),
            ("ewo", ewo_hbm, ewo_ref),
            ("eg", eg_hbm, eg_ref),
            ("ecot", ecot_hbm, ecot_ref),
        )
    ):
        loads[name] = pltpu.make_async_copy(src, dst, load_sem.at[i])
    tile = sloc_ref.shape[1]
    me = lax.axis_index("row")
    group = 4 * tile
    steps = [s for s in (1, 2)]
    hops = [0, stride, 2 * stride, 0, 1, 2]
    remote = (1, 2, 4, 5)
    outer = n // INNER
    ia, ib = lax.rem(me, INNER), me // INNER

    def at(offset):
        return lax.rem(me + offset % n, n)

    def inner_peer(i):
        return ib * INNER + lax.rem(ia + i, INNER)

    def outer_peer(i):
        return lax.rem(ib + i, outer) * INNER + ia

    partners = [at(o) for o in sorted({k for s in (1, 2) for d in (1, stride) for k in (s * d % n, -s * d % n)})]
    if fused:
        partners += [inner_peer(i) for i in range(1, INNER)]
        partners += [outer_peer(i) for i in range(1, outer)]
    barrier = pltpu.get_barrier_semaphore()
    for p in partners:
        pl.semaphore_signal(barrier, inc=1, device_id={"row": p}, device_id_type=pl.DeviceIdType.MESH)

    for c in loads.values():
        c.start()

    used = [0]

    def remote_copy(src, dst, target):
        k = used[0]
        used[0] += 1
        copy = pltpu.make_async_remote_copy(
            src_ref=src,
            dst_ref=dst,
            send_sem=send_sem.at[k],
            recv_sem=recv_sem.at[k],
            device_id={"row": target},
            device_id_type=pl.DeviceIdType.MESH,
        )
        copy.start()
        return copy

    class Relayed:
        def __init__(self, src, hold, dst, via, direct, first, second):
            k = used[0]
            used[0] += 3
            self.src, self.hold, self.dst, self.k, self.via = src, hold, dst, k, via
            self.direct, self.first, self.second = direct, first, second

            @pl.when(via)
            def _():
                self.hop().start()

            @pl.when(jnp.logical_not(via))
            def _():
                self.straight().start()

        def make(self, src, dst, offset, send, recv):
            return pltpu.make_async_remote_copy(
                src_ref=src,
                dst_ref=dst,
                send_sem=send_sem.at[send],
                recv_sem=recv_sem.at[recv],
                device_id={"row": at(offset)},
                device_id_type=pl.DeviceIdType.MESH,
            )

        def hop(self):
            return self.make(self.src, self.hold, self.first, self.k, self.k)

        def straight(self):
            return self.make(self.src, self.dst, self.direct, self.k + 1, self.k + 1)

        def onward(self):
            return self.make(self.hold, self.dst, self.second, self.k + 2, self.k + 1)

        def forward(self):
            @pl.when(jnp.logical_not(self.via))
            def _():
                self.hop().wait_recv()
                self.onward().start()

        def wait(self):
            self.straight().wait_recv()

            @pl.when(self.via)
            def _():
                self.hop().wait_send()

            @pl.when(jnp.logical_not(self.via))
            def _():
                self.straight().wait_send()
                self.onward().wait_send()

    relay = fused and stride == 2
    x_low = lax.rem(me // 2, 2) == 0
    x_high = jnp.logical_not(x_low)

    loads["sloc"].wait()
    loads["rloc"].wait()
    for side, (loc, slot) in enumerate(((sloc_ref, sslot_ref), (rloc_ref, rslot_ref))):
        tiles = [loc[j : j + 1, :] for j in range(6)]
        none = jnp.full((1, tile), -1, jnp.int32)
        for s in range(3):
            k = side * 3 + s
            lead = lax.select(slot[0] == s, tiles[0], lax.select(slot[1] == s, tiles[1], tiles[2]))
            req[k, :, 0:tile] = lead
            for j in range(3):
                req[k, :, tile * (j + 1) : tile * (j + 2)] = lax.select(slot[3 + j] == s, tiles[3 + j], none)

    pl.semaphore_wait(barrier, len(partners))
    asks = {k: remote_copy(req.at[k], req_in.at[k], at(hops[k])) for k in remote}

    def make_onehot(k, index_ref):
        index = index_ref[k]

        def rows(i, carry):
            r = pl.multiple_of(i * 128, 128)
            ids = lax.broadcasted_iota(jnp.int32, (128, group), 0) + r
            onehot[k, pl.ds(r, 128), :] = (ids == index).astype(F32).astype(BF16)
            return carry

        lax.fori_loop(0, nb // 128, rows, 0)

    loads["x"].wait()
    for k in (0, 3):
        make_onehot(k, req)
        lat_in[k] = mm_tn(onehot[k], x_ref[...]).astype(BF16)
    lats = {}
    for k in (1, 2, 5, 4):
        asks[k].wait()
        make_onehot(k, req_in)
        lat_out[k] = mm_tn(onehot[k], x_ref[...]).astype(BF16)
        if relay and k == 1:
            lats[k] = Relayed(lat_out.at[k], hold.at[0], lat_in.at[k], x_low, -2, 2, -4)
        else:
            lats[k] = remote_copy(lat_out.at[k], lat_in.at[k], at(-hops[k]))

    gain_acc[...] = jnp.zeros_like(gain_acc)
    for name in ("nwi", "agg", "nwo", "ng", "ncot"):
        loads[name].wait()

    def node_rows(i, carry):
        r = pl.ds(pl.multiple_of(i * 256, 256), 256)
        pre = mm(x_ref[r, :], nwi_ref[0:h, :]) + mm(agg_ref[r, :], nwi_ref[h:, :])
        sig = lax.logistic(pre)
        act = (pre * sig).astype(BF16)
        n_act[r, :] = act
        cot = ncot_ref[r, :].astype(F32)
        dout, gg = norm_backward(mm(act, nwo_ref[...]), cot, ng_ref[...])
        gain_acc[8:9, :] += gg
        n_dout[r, :] = dout
        dpre = (mm_nt(dout, nwo_ref[...]) * sig * (1.0 + pre * (1.0 - sig))).astype(BF16)
        n_dpre[r, :] = dpre
        n_agg[r, :] = mm_nt(dpre, nwi_ref[h:, :]).astype(BF16)
        n_base[r, :] = cot + mm_nt(dpre, nwi_ref[0:h, :])
        return carry

    lax.fori_loop(0, nb // 256, node_rows, 0)
    if relay:
        lats[1].forward()
    aggs = {}
    for s in (2, 1):
        agg_out[s] = mm_tn(onehot[3 + s], n_agg[...]).astype(BF16)
        if relay and s == 2:
            aggs[s] = Relayed(agg_out.at[s], hold.at[1], agg_in.at[s], x_low, -2, 2, -4)
        else:
            aggs[s] = remote_copy(agg_out.at[s], agg_in.at[s], at(-s))
    agg_in[0] = mm_tn(onehot[3], n_agg[...]).astype(BF16)

    def rows_of(lo, rows, part):
        return pl.ds(pl.multiple_of(lo + part * rows, 16), rows)

    def give_weights(outs, rows):
        split = outs[0].shape[0]
        outs[0][...] = rows(0, split)
        outs[1][...] = rows(split, split + h)

    class Sum:
        def __init__(self, lo, total, scale, full, outs):
            self.outs = outs
            self.lo, self.total, self.scale, self.full = lo, total, scale, full
            self.q = total // INNER
            self.e = self.q // outer
            self.qlo, self.elo = lo // INNER, lo // INNER // outer

        def start_a(self):
            w_src[self.lo : self.lo + self.total, :] = self.full[...].astype(BF16)
            self.copies = [
                remote_copy(
                    w_src.at[rows_of(self.lo, self.q, lax.rem(ia + i, INNER)), :],
                    w_a.at[i - 1, pl.ds(self.qlo, self.q), :],
                    inner_peer(i),
                )
                for i in range(1, INNER)
            ]

        def start_b(self):
            for c in self.copies:
                c.wait()
            total = self.full[rows_of(0, self.q, ia), :]
            mine = pl.ds(self.qlo, self.q)
            for i in range(INNER - 1):
                total = total + w_a[i, mine, :].astype(F32)
            w_sum[mine, :] = total
            w_b_src[mine, :] = total.astype(BF16)
            self.copies = [
                remote_copy(
                    w_b_src.at[rows_of(self.qlo, self.e, lax.rem(ib + i, outer)), :],
                    w_b.at[i - 1, pl.ds(self.elo, self.e), :],
                    outer_peer(i),
                )
                for i in range(1, outer)
            ]

        def start_c(self):
            for c in self.copies:
                c.wait()
            total = w_sum[rows_of(self.qlo, self.e, ib), :]
            for i in range(outer - 1):
                total = total + w_b[i, pl.ds(self.elo, self.e), :].astype(F32)
            piece = pl.ds(pl.multiple_of(self.lo + ia * self.q + ib * self.e, 16), self.e)
            w_fin[piece, :] = (total * self.scale).astype(BF16)
            self.copies = [
                remote_copy(w_fin.at[piece, :], w_fin.at[piece, :], outer_peer(i)) for i in range(1, outer)
            ]

        def start_d(self):
            for c in self.copies:
                c.wait()
            piece = rows_of(self.lo, self.q, ia)
            self.copies = [
                remote_copy(w_fin.at[piece, :], w_fin.at[piece, :], inner_peer(i)) for i in range(1, INNER)
            ]

        def finish(self):
            for c in self.copies:
                c.wait()
            give_weights(self.outs, lambda a, b: w_fin[self.lo + a : self.lo + b, :])

    n_total = ngw_ref.shape[0]
    e_total = egw_ref.shape[0]
    edge_sum = Sum(0, e_total, edge_scale, egw_ref, (egwi_out, egwo_out))
    node_sum = Sum(e_total, n_total, node_scale, ngw_ref, (ngwi_out, ngwo_out))
    ngw_ref[0:h, :] = mm_tn(x_ref[...], n_dpre[...])
    ngw_ref[h : 2 * h, :] = mm_tn(agg_ref[...], n_dpre[...])
    ngw_ref[2 * h :, :] = mm_tn(n_act[...], n_dout[...])
    if fused:
        node_sum.start_a()

    for name in ("e", "ewi", "ewo", "eg", "ecot"):
        loads[name].wait()
    def unpack(side, slot, buffer, table):
        for j in range(6):
            lo = 0 if j < 3 else tile * (j - 2)
            options = [buffer[side * 3 + s, lo : lo + tile, :] for s in range(3)]
            table[j * tile : (j + 1) * tile, :] = pick(slot[j], options)

    for k in (2, 1):
        lats[k].wait()
    unpack(0, sslot_ref, lat_in, snd)
    if relay:
        aggs[2].forward()
    for k in (5, 4):
        lats[k].wait()
    unpack(1, rslot_ref, lat_in, rcv)
    if fused:
        node_sum.start_b()

    def edge_forward(i, carry):
        r = pl.ds(pl.multiple_of(i * 256, 256), 256)
        pre = mm(e_ref[r, :], ewi_ref[0:h, :]) + mm(snd[r, :], ewi_ref[h : 2 * h, :]) + mm(rcv[r, :], ewi_ref[2 * h :, :])
        e_pre[r, :] = pre
        act = (pre * lax.logistic(pre)).astype(BF16)
        e_act[r, :] = act
        e_out[r, :] = mm(act, ewo_ref[...])
        return carry

    lax.fori_loop(0, edges // 256, edge_forward, 0)
    if fused:
        node_sum.start_c()
    for s in (2, 1):
        aggs[s].wait()
    unpack(0, rslot_ref, agg_in, e_dpre)
    live_rows = count_ref[0] * tile

    def edge_backward(i, carry):
        lo = pl.multiple_of(i * 256, 256)
        r = pl.ds(lo, 256)
        live = (lax.broadcasted_iota(jnp.int32, (256, h), 0) + lo) < live_rows
        cot = jnp.where(live, ecot_ref[r, :].astype(F32) + e_dpre[r, :].astype(F32), 0.0)
        dout, gg = norm_backward(e_out[r, :], cot, eg_ref[...])
        gain_acc[0:1, :] += gg
        e_dout[r, :] = dout
        pre = e_pre[r, :]
        sig = lax.logistic(pre)
        dpre = (mm_nt(dout, ewo_ref[...]) * sig * (1.0 + pre * (1.0 - sig))).astype(BF16)
        e_dpre[r, :] = dpre
        egrad_ref[r, :] = (cot + mm_nt(dpre, ewi_ref[0:h, :])).astype(BF16)
        e_out[r, :] = mm_nt(dpre, ewi_ref[h : 2 * h, :])
        e_pre[r, :] = mm_nt(dpre, ewi_ref[2 * h :, :])
        return carry

    lax.fori_loop(0, edges // 256, edge_backward, 0)

    rets = {}
    for k in (5, 1, 2, 4, 0, 3):
        s = k % 3
        grads, slot = (e_out, sslot_ref) if k < 3 else (e_pre, rslot_ref)
        target = ret_in if s == 0 else ret_out
        lead = [grads[j * tile : (j + 1) * tile, :] for j in range(3)]
        lead = lax.select(slot[0] == s, lead[0], lax.select(slot[1] == s, lead[1], lead[2]))
        target[k, 0:tile, :] = lead.astype(BF16)
        target[k, tile:, :] = grads[3 * tile :, :].astype(BF16)
        if relay and k == 5:
            rets[k] = Relayed(ret_out.at[k], hold.at[2], ret_in.at[k], x_high, 2, -2, 4)
        elif s:
            rets[k] = remote_copy(ret_out.at[k], ret_in.at[k], at(hops[k]))

    if fused:
        node_sum.start_d()
    egw_ref[0:h, :] = mm_tn(e_ref[...], e_dpre[...])
    egw_ref[h : 2 * h, :] = mm_tn(snd[...], e_dpre[...])
    egw_ref[2 * h : 3 * h, :] = mm_tn(rcv[...], e_dpre[...])
    egw_ref[3 * h :, :] = mm_tn(e_act[...], e_dout[...])
    if fused:
        edge_sum.start_a()
        g_a[ia] = gain_acc[...]
        gains = [remote_copy(gain_acc, g_a.at[ia], inner_peer(i)) for i in range(1, INNER)]

    n_base[...] += mm(onehot[0], ret_in[0]) + mm(onehot[3], ret_in[3])
    if relay:
        rets[5].forward()
    if fused:
        node_sum.finish()
        edge_sum.start_b()
        for c in gains:
            c.wait()
        g_sum = g_a[0]
        for i in range(1, INNER):
            g_sum = g_sum + g_a[i]
        gain_acc[...] = g_sum
        g_b[ib] = g_sum
        gains = [remote_copy(gain_acc, g_b.at[ib], outer_peer(i)) for i in range(1, outer)]
        edge_sum.start_c()
    for k in (1, 4):
        rets[k].wait()
    n_base[...] += mm(onehot[1], ret_in[1]) + mm(onehot[4], ret_in[4])
    if fused:
        edge_sum.start_d()
    for k in (2, 5):
        rets[k].wait()
    total = n_base[...] + mm(onehot[2], ret_in[2]) + mm(onehot[5], ret_in[5])
    ngrad_ref[...] = total.astype(BF16)
    if fused:
        for c in gains:
            c.wait()
        g_sum = g_b[0]
        for i in range(1, outer):
            g_sum = g_sum + g_b[i]
        egain_out[...] = g_sum[0:1, :] * edge_scale
        ngain_out[...] = g_sum[8:9, :] * node_scale
        edge_sum.finish()
    else:
        egain_out[...] = gain_acc[0:1, :] * edge_scale
        ngain_out[...] = gain_acc[8:9, :] * node_scale
        give_weights(edge_sum.outs, lambda a, b: egw_ref[a:b, :] * edge_scale)
        give_weights(node_sum.outs, lambda a, b: ngw_ref[a:b, :] * node_scale)


def on_device(
    node_latent,
    agg_saved,
    node_cot,
    edge_latent,
    edge_cot,
    send_local,
    recv_local,
    send_slot,
    recv_slot,
    tile_count,
    edge_w_in,
    edge_w_out,
    edge_gain,
    node_w_in,
    node_w_out,
    node_gain,
):
    nb, h = node_latent.shape
    edges = edge_latent.shape[0]
    tile_total, tile = send_local.shape
    n = lax.axis_size("row")
    stride = n // 8
    node_scale = (nb * n) ** (-0.5)
    edge_scale = (edges * n) ** (-0.5)
    outer = n // INNER
    fused = n % INNER == 0 and 3 * h % (INNER * outer * 16) == 0 and 4 * h % (INNER * outer * 16) == 0
    levels = outer if fused else 2
    group = 4 * tile
    weights = 7 * h
    vmem = pl.BlockSpec(memory_space=pltpu.VMEM)
    smem = pl.BlockSpec(memory_space=pltpu.SMEM)
    copies = 20 + (2 * (2 * (INNER - 1) + 2 * (outer - 1)) + INNER - 1 + outer - 1 if fused else 0)
    anywhere = pl.BlockSpec(memory_space=pl.ANY)
    summed = BF16 if fused else F32
    node_grad, edge_grad, *sums = pl.pallas_call(
        functools.partial(layer_kernel, n, stride, fused, node_scale, edge_scale),
        out_shape=(
            jax.ShapeDtypeStruct((nb, h), BF16),
            jax.ShapeDtypeStruct((edges, h), BF16),
            jax.ShapeDtypeStruct((3 * h, h), summed),
            jax.ShapeDtypeStruct((h, h), summed),
            jax.ShapeDtypeStruct((2 * h, h), summed),
            jax.ShapeDtypeStruct((h, h), summed),
            jax.ShapeDtypeStruct((1, h), F32),
            jax.ShapeDtypeStruct((1, h), F32),
        ),
        in_specs=[anywhere] * 7 + [smem] * 3 + [anywhere] * 6,
        out_specs=(vmem,) * 8,
        scratch_shapes=[
            pltpu.VMEM((nb, h), BF16),
            pltpu.VMEM((nb, h), BF16),
            pltpu.VMEM((nb, h), BF16),
            pltpu.VMEM((edges, h), BF16),
            pltpu.VMEM((edges, h), BF16),
            pltpu.VMEM((tile_total, tile), jnp.int32),
            pltpu.VMEM((tile_total, tile), jnp.int32),
            pltpu.VMEM((3 * h, h), BF16),
            pltpu.VMEM((h, h), BF16),
            pltpu.VMEM((1, h), F32),
            pltpu.VMEM((2 * h, h), BF16),
            pltpu.VMEM((h, h), BF16),
            pltpu.VMEM((1, h), F32),
            pltpu.VMEM((4 * h, h), F32),
            pltpu.VMEM((3 * h, h), F32),
            pltpu.SemaphoreType.DMA((13,)),
            pltpu.VMEM((6, 1, group), jnp.int32),
            pltpu.VMEM((6, 1, group), jnp.int32),
            pltpu.VMEM((6, nb, group), BF16),
            pltpu.VMEM((6, group, h), BF16),
            pltpu.VMEM((6, group, h), BF16),
            pltpu.VMEM((3, group, h), BF16),
            pltpu.VMEM((3, group, h), BF16),
            pltpu.VMEM((6, group, h), BF16),
            pltpu.VMEM((6, group, h), BF16),
            pltpu.VMEM((nb, h), BF16),
            pltpu.VMEM((nb, h), BF16),
            pltpu.VMEM((nb, h), BF16),
            pltpu.VMEM((nb, h), BF16),
            pltpu.VMEM((nb, h), F32),
            pltpu.VMEM((edges, h), BF16),
            pltpu.VMEM((edges, h), BF16),
            pltpu.VMEM((edges, h), F32),
            pltpu.VMEM((edges, h), BF16),
            pltpu.VMEM((edges, h), F32),
            pltpu.VMEM((edges, h), BF16),
            pltpu.VMEM((edges, h), BF16),
            pltpu.VMEM((16, h), F32),
            pltpu.VMEM((weights, h), BF16),
            pltpu.VMEM((INNER - 1, weights // INNER, h), BF16),
            pltpu.VMEM((weights // INNER, h), F32),
            pltpu.VMEM((weights // INNER, h), BF16),
            pltpu.VMEM((levels - 1, weights // INNER // levels, h), BF16),
            pltpu.VMEM((weights, h), BF16),
            pltpu.VMEM((INNER, 16, h), F32),
            pltpu.VMEM((levels, 16, h), F32),
            pltpu.VMEM((3, group, h), BF16),
            pltpu.SemaphoreType.DMA((copies,)),
            pltpu.SemaphoreType.DMA((copies,)),
        ],
        compiler_params=pltpu.CompilerParams(
            collective_id=0, has_side_effects=True, vmem_limit_bytes=60 * 1024 * 1024
        ),
        cost_estimate=pl.CostEstimate(flops=7 * 10**9, bytes_accessed=8 * 10**6, transcendentals=10**6),
    )(
        node_latent,
        agg_saved,
        node_cot,
        edge_latent,
        edge_cot,
        send_local,
        recv_local,
        send_slot,
        recv_slot,
        tile_count,
        edge_w_in,
        edge_w_out,
        edge_gain[None, :],
        node_w_in,
        node_w_out,
        node_gain[None, :],
    )
    if not fused:
        sums = lax.psum(tuple(sums), "row")
    egwi, egwo, ngwi, ngwo, egain, ngain = [v.astype(F32) for v in sums]
    return (node_grad, edge_grad, egwi, egwo, egain[0], ngwi, ngwo, ngain[0])


def solution(mesh):
    placed = (P(("parts", "row"), None),) * 7 + (P(("parts", "row")),) * 3 + (P(),) * 6
    return jax.shard_map(
        on_device,
        mesh=mesh,
        in_specs=placed,
        out_specs=(
            P(("parts", "row"), None),
            P(("parts", "row"), None),
            P("parts", None),
            P("parts", None),
            P("parts"),
            P("parts", None),
            P("parts", None),
            P("parts"),
        ),
        check_vma=False,
    )
```

```python
import functools
import jax
import jax.numpy as jnp
from jax import lax
from jax.experimental import pallas as pl
from jax.experimental.pallas import tpu as pltpu
from jax.sharding import PartitionSpec as P

EPSILON = 1e-05
F32 = jnp.float32
BF16 = jnp.bfloat16
INNER = 4


def mm(a, b):
    return jnp.dot(a, b, preferred_element_type=F32)


def mm_nt(a, b):
    return lax.dot_general(a, b, (((1,), (1,)), ((), ())), preferred_element_type=F32)


def mm_tn(a, b):
    return lax.dot_general(a, b, (((0,), (0,)), ((), ())), preferred_element_type=F32)


def norm_backward(output, cotangent, gain):
    row_mean = jnp.mean(output, axis=-1, keepdims=True)
    centred = output - row_mean
    inverse = lax.rsqrt(jnp.mean(centred * centred, axis=-1, keepdims=True) + EPSILON)
    normed = centred * inverse
    grad_gain = jnp.sum(cotangent * normed, axis=0, keepdims=True)
    scaled = cotangent * gain
    out_grad = inverse * (
        scaled
        - jnp.mean(scaled, axis=-1, keepdims=True)
        - normed * jnp.mean(scaled * normed, axis=-1, keepdims=True)
    )
    return out_grad.astype(BF16), grad_gain


def pick(slot, options):
    return lax.select(slot == 0, options[0], lax.select(slot == 1, options[1], options[2]))


def layer_kernel(
    n,
    stride,
    fused,
    node_scale,
    edge_scale,
    x_hbm,
    agg_hbm,
    ncot_hbm,
    e_hbm,
    ecot_hbm,
    sloc_hbm,
    rloc_hbm,
    sslot_ref,
    rslot_ref,
    count_ref,
    ewi_hbm,
    ewo_hbm,
    eg_hbm,
    nwi_hbm,
    nwo_hbm,
    ng_hbm,
    ngrad_ref,
    egrad_ref,
    egwi_out,
    egwo_out,
    ngwi_out,
    ngwo_out,
    egain_out,
    ngain_out,
    x_ref,
    agg_ref,
    ncot_ref,
    e_ref,
    ecot_ref,
    sloc_ref,
    rloc_ref,
    ewi_ref,
    ewo_ref,
    eg_ref,
    nwi_ref,
    nwo_ref,
    ng_ref,
    egw_ref,
    ngw_ref,
    load_sem,
    req,
    req_in,
    onehot,
    lat_out,
    lat_in,
    agg_out,
    agg_in,
    ret_out,
    ret_in,
    n_act,
    n_dout,
    n_dpre,
    n_agg,
    n_base,
    snd,
    rcv,
    e_pre,
    e_act,
    e_out,
    e_dout,
    e_dpre,
    gain_acc,
    w_src,
    w_a,
    w_sum,
    w_b_src,
    w_b,
    w_fin,
    g_a,
    g_b,
    hold,
    send_sem,
    recv_sem,
):
    nb, h = x_ref.shape
    edges = e_ref.shape[0]
    loads = {}
    for i, (name, src, dst) in enumerate(
        (
            ("sloc", sloc_hbm, sloc_ref),
            ("rloc", rloc_hbm, rloc_ref),
            ("x", x_hbm, x_ref),
            ("nwi", nwi_hbm, nwi_ref),
            ("agg", agg_hbm, agg_ref),
            ("nwo", nwo_hbm, nwo_ref),
            ("ng", ng_hbm, ng_ref),
            ("ncot", ncot_hbm, ncot_ref),
            ("e", e_hbm, e_ref),
            ("ewi", ewi_hbm, ewi_ref),
            ("ewo", ewo_hbm, ewo_ref),
            ("eg", eg_hbm, eg_ref),
            ("ecot", ecot_hbm, ecot_ref),
        )
    ):
        loads[name] = pltpu.make_async_copy(src, dst, load_sem.at[i])
    tile = sloc_ref.shape[1]
    me = lax.axis_index("row")
    group = 4 * tile
    steps = [s for s in (1, 2)]
    hops = [0, stride, 2 * stride, 0, 1, 2]
    remote = (1, 2, 4, 5)
    outer = n // INNER
    ia, ib = lax.rem(me, INNER), me // INNER

    def at(offset):
        return lax.rem(me + offset % n, n)

    def inner_peer(i):
        return ib * INNER + lax.rem(ia + i, INNER)

    def outer_peer(i):
        return lax.rem(ib + i, outer) * INNER + ia

    partners = [at(o) for o in sorted({k for s in (1, 2) for d in (1, stride) for k in (s * d % n, -s * d % n)})]
    if fused:
        partners += [inner_peer(i) for i in range(1, INNER)]
        partners += [outer_peer(i) for i in range(1, outer)]
    barrier = pltpu.get_barrier_semaphore()
    for p in partners:
        pl.semaphore_signal(barrier, inc=1, device_id={"row": p}, device_id_type=pl.DeviceIdType.MESH)

    for c in loads.values():
        c.start()

    used = [0]

    def remote_copy(src, dst, target):
        k = used[0]
        used[0] += 1
        copy = pltpu.make_async_remote_copy(
            src_ref=src,
            dst_ref=dst,
            send_sem=send_sem.at[k],
            recv_sem=recv_sem.at[k],
            device_id={"row": target},
            device_id_type=pl.DeviceIdType.MESH,
        )
        copy.start()
        return copy

    class Relayed:
        def __init__(self, src, hold, dst, via, direct, first, second):
            k = used[0]
            used[0] += 3
            self.src, self.hold, self.dst, self.k, self.via = src, hold, dst, k, via
            self.direct, self.first, self.second = direct, first, second

            @pl.when(via)
            def _():
                self.hop().start()

            @pl.when(jnp.logical_not(via))
            def _():
                self.straight().start()

        def make(self, src, dst, offset, send, recv):
            return pltpu.make_async_remote_copy(
                src_ref=src,
                dst_ref=dst,
                send_sem=send_sem.at[send],
                recv_sem=recv_sem.at[recv],
                device_id={"row": at(offset)},
                device_id_type=pl.DeviceIdType.MESH,
            )

        def hop(self):
            return self.make(self.src, self.hold, self.first, self.k, self.k)

        def straight(self):
            return self.make(self.src, self.dst, self.direct, self.k + 1, self.k + 1)

        def onward(self):
            return self.make(self.hold, self.dst, self.second, self.k + 2, self.k + 1)

        def forward(self):
            @pl.when(jnp.logical_not(self.via))
            def _():
                self.hop().wait_recv()
                self.onward().start()

        def wait(self):
            self.straight().wait_recv()

            @pl.when(self.via)
            def _():
                self.hop().wait_send()

            @pl.when(jnp.logical_not(self.via))
            def _():
                self.straight().wait_send()
                self.onward().wait_send()

    relay = fused and stride == 2
    x_low = lax.rem(me // 2, 2) == 0
    x_high = jnp.logical_not(x_low)

    loads["sloc"].wait()
    loads["rloc"].wait()
    for side, (loc, slot) in enumerate(((sloc_ref, sslot_ref), (rloc_ref, rslot_ref))):
        tiles = [loc[j : j + 1, :] for j in range(6)]
        none = jnp.full((1, tile), -1, jnp.int32)
        for s in range(3):
            k = side * 3 + s
            lead = lax.select(slot[0] == s, tiles[0], lax.select(slot[1] == s, tiles[1], tiles[2]))
            req[k, :, 0:tile] = lead
            for j in range(3):
                req[k, :, tile * (j + 1) : tile * (j + 2)] = lax.select(slot[3 + j] == s, tiles[3 + j], none)

    pl.semaphore_wait(barrier, len(partners))
    asks = {k: remote_copy(req.at[k], req_in.at[k], at(hops[k])) for k in remote}

    def make_onehot(k, index_ref):
        index = index_ref[k]

        def rows(i, carry):
            r = pl.multiple_of(i * 128, 128)
            ids = lax.broadcasted_iota(jnp.int32, (128, group), 0) + r
            onehot[k, pl.ds(r, 128), :] = (ids == index).astype(F32).astype(BF16)
            return carry

        lax.fori_loop(0, nb // 128, rows, 0)

    loads["x"].wait()
    for k in (0, 3):
        make_onehot(k, req)
        lat_in[k] = mm_tn(onehot[k], x_ref[...]).astype(BF16)
    lats = {}
    for k in (1, 2, 5, 4):
        asks[k].wait()
        make_onehot(k, req_in)
        lat_out[k] = mm_tn(onehot[k], x_ref[...]).astype(BF16)
        if relay and k == 1:
            lats[k] = Relayed(lat_out.at[k], hold.at[0], lat_in.at[k], x_low, -2, 2, -4)
        else:
            lats[k] = remote_copy(lat_out.at[k], lat_in.at[k], at(-hops[k]))

    gain_acc[...] = jnp.zeros_like(gain_acc)
    for name in ("nwi", "agg", "nwo", "ng", "ncot"):
        loads[name].wait()

    def node_rows(i, carry):
        r = pl.ds(pl.multiple_of(i * 256, 256), 256)
        pre = mm(x_ref[r, :], nwi_ref[0:h, :]) + mm(agg_ref[r, :], nwi_ref[h:, :])
        sig = lax.logistic(pre)
        act = (pre * sig).astype(BF16)
        n_act[r, :] = act
        cot = ncot_ref[r, :].astype(F32)
        dout, gg = norm_backward(mm(act, nwo_ref[...]), cot, ng_ref[...])
        gain_acc[8:9, :] += gg
        n_dout[r, :] = dout
        dpre = (mm_nt(dout, nwo_ref[...]) * sig * (1.0 + pre * (1.0 - sig))).astype(BF16)
        n_dpre[r, :] = dpre
        n_agg[r, :] = mm_nt(dpre, nwi_ref[h:, :]).astype(BF16)
        n_base[r, :] = cot + mm_nt(dpre, nwi_ref[0:h, :])
        return carry

    lax.fori_loop(0, nb // 256, node_rows, 0)
    if relay:
        lats[1].forward()
    aggs = {}
    for s in (2, 1):
        agg_out[s] = mm_tn(onehot[3 + s], n_agg[...]).astype(BF16)
        if relay and s == 2:
            aggs[s] = Relayed(agg_out.at[s], hold.at[1], agg_in.at[s], x_low, -2, 2, -4)
        else:
            aggs[s] = remote_copy(agg_out.at[s], agg_in.at[s], at(-s))
    agg_in[0] = mm_tn(onehot[3], n_agg[...]).astype(BF16)

    def rows_of(lo, rows, part):
        return pl.ds(pl.multiple_of(lo + part * rows, 16), rows)

    def give_weights(outs, rows):
        split = outs[0].shape[0]
        outs[0][...] = rows(0, split)
        outs[1][...] = rows(split, split + h)

    class Sum:
        def __init__(self, lo, total, scale, full, outs):
            self.outs = outs
            self.lo, self.total, self.scale, self.full = lo, total, scale, full
            self.q = total // INNER
            self.e = self.q // outer
            self.qlo, self.elo = lo // INNER, lo // INNER // outer

        def start_a(self):
            w_src[self.lo : self.lo + self.total, :] = self.full[...].astype(BF16)
            self.copies = [
                remote_copy(
                    w_src.at[rows_of(self.lo, self.q, lax.rem(ia + i, INNER)), :],
                    w_a.at[i - 1, pl.ds(self.qlo, self.q), :],
                    inner_peer(i),
                )
                for i in range(1, INNER)
            ]

        def start_b(self):
            for c in self.copies:
                c.wait()
            total = self.full[rows_of(0, self.q, ia), :]
            mine = pl.ds(self.qlo, self.q)
            for i in range(INNER - 1):
                total = total + w_a[i, mine, :].astype(F32)
            w_sum[mine, :] = total
            w_b_src[mine, :] = total.astype(BF16)
            self.copies = [
                remote_copy(
                    w_b_src.at[rows_of(self.qlo, self.e, lax.rem(ib + i, outer)), :],
                    w_b.at[i - 1, pl.ds(self.elo, self.e), :],
                    outer_peer(i),
                )
                for i in range(1, outer)
            ]

        def start_c(self):
            for c in self.copies:
                c.wait()
            total = w_sum[rows_of(self.qlo, self.e, ib), :]
            for i in range(outer - 1):
                total = total + w_b[i, pl.ds(self.elo, self.e), :].astype(F32)
            piece = pl.ds(pl.multiple_of(self.lo + ia * self.q + ib * self.e, 16), self.e)
            w_fin[piece, :] = (total * self.scale).astype(BF16)
            self.copies = [
                remote_copy(w_fin.at[piece, :], w_fin.at[piece, :], outer_peer(i)) for i in range(1, outer)
            ]

        def start_d(self):
            for c in self.copies:
                c.wait()
            piece = rows_of(self.lo, self.q, ia)
            self.copies = [
                remote_copy(w_fin.at[piece, :], w_fin.at[piece, :], inner_peer(i)) for i in range(1, INNER)
            ]

        def finish(self):
            for c in self.copies:
                c.wait()
            give_weights(self.outs, lambda a, b: w_fin[self.lo + a : self.lo + b, :])

    n_total = ngw_ref.shape[0]
    e_total = egw_ref.shape[0]
    edge_sum = Sum(0, e_total, edge_scale, egw_ref, (egwi_out, egwo_out))
    node_sum = Sum(e_total, n_total, node_scale, ngw_ref, (ngwi_out, ngwo_out))
    ngw_ref[0:h, :] = mm_tn(x_ref[...], n_dpre[...])
    ngw_ref[h : 2 * h, :] = mm_tn(agg_ref[...], n_dpre[...])
    ngw_ref[2 * h :, :] = mm_tn(n_act[...], n_dout[...])
    if fused:
        node_sum.start_a()

    for name in ("e", "ewi", "ewo", "eg", "ecot"):
        loads[name].wait()
    def unpack(side, slot, buffer, table):
        for j in range(6):
            lo = 0 if j < 3 else tile * (j - 2)
            options = [buffer[side * 3 + s, lo : lo + tile, :] for s in range(3)]
            table[j * tile : (j + 1) * tile, :] = pick(slot[j], options)

    for k in (2, 1):
        lats[k].wait()
    unpack(0, sslot_ref, lat_in, snd)
    if relay:
        aggs[2].forward()
    for k in (5, 4):
        lats[k].wait()
    unpack(1, rslot_ref, lat_in, rcv)
    if fused:
        node_sum.start_b()

    def edge_forward(i, carry):
        r = pl.ds(pl.multiple_of(i * 256, 256), 256)
        pre = mm(e_ref[r, :], ewi_ref[0:h, :]) + mm(snd[r, :], ewi_ref[h : 2 * h, :]) + mm(rcv[r, :], ewi_ref[2 * h :, :])
        e_pre[r, :] = pre
        act = (pre * lax.logistic(pre)).astype(BF16)
        e_act[r, :] = act
        e_out[r, :] = mm(act, ewo_ref[...])
        return carry

    lax.fori_loop(0, edges // 256, edge_forward, 0)
    if fused:
        node_sum.start_c()
    for s in (2, 1):
        aggs[s].wait()
    unpack(0, rslot_ref, agg_in, e_dpre)
    if fused:
        node_sum.start_d()
    live_rows = count_ref[0] * tile

    def edge_backward(i, carry):
        lo = pl.multiple_of(i * 256, 256)
        r = pl.ds(lo, 256)
        live = (lax.broadcasted_iota(jnp.int32, (256, h), 0) + lo) < live_rows
        cot = jnp.where(live, ecot_ref[r, :].astype(F32) + e_dpre[r, :].astype(F32), 0.0)
        dout, gg = norm_backward(e_out[r, :], cot, eg_ref[...])
        gain_acc[0:1, :] += gg
        e_dout[r, :] = dout
        pre = e_pre[r, :]
        sig = lax.logistic(pre)
        dpre = (mm_nt(dout, ewo_ref[...]) * sig * (1.0 + pre * (1.0 - sig))).astype(BF16)
        e_dpre[r, :] = dpre
        egrad_ref[r, :] = (cot + mm_nt(dpre, ewi_ref[0:h, :])).astype(BF16)
        e_out[r, :] = mm_nt(dpre, ewi_ref[h : 2 * h, :])
        e_pre[r, :] = mm_nt(dpre, ewi_ref[2 * h :, :])
        return carry

    lax.fori_loop(0, edges // 256, edge_backward, 0)

    egw_ref[0:h, :] = mm_tn(e_ref[...], e_dpre[...])
    egw_ref[h : 2 * h, :] = mm_tn(snd[...], e_dpre[...])
    egw_ref[2 * h : 3 * h, :] = mm_tn(rcv[...], e_dpre[...])
    egw_ref[3 * h :, :] = mm_tn(e_act[...], e_dout[...])
    if fused:
        edge_sum.start_a()
        g_a[ia] = gain_acc[...]
        gains = [remote_copy(gain_acc, g_a.at[ia], inner_peer(i)) for i in range(1, INNER)]

    rets = {}
    for k in (5, 1, 2, 4, 0, 3):
        s = k % 3
        grads, slot = (e_out, sslot_ref) if k < 3 else (e_pre, rslot_ref)
        target = ret_in if s == 0 else ret_out
        lead = [grads[j * tile : (j + 1) * tile, :] for j in range(3)]
        lead = lax.select(slot[0] == s, lead[0], lax.select(slot[1] == s, lead[1], lead[2]))
        target[k, 0:tile, :] = lead.astype(BF16)
        target[k, tile:, :] = grads[3 * tile :, :].astype(BF16)
        if relay and k == 5:
            rets[k] = Relayed(ret_out.at[k], hold.at[2], ret_in.at[k], x_high, 2, -2, 4)
        elif s:
            rets[k] = remote_copy(ret_out.at[k], ret_in.at[k], at(hops[k]))

    n_base[...] += mm(onehot[0], ret_in[0]) + mm(onehot[3], ret_in[3])
    if relay:
        rets[5].forward()
    if fused:
        edge_sum.start_b()
        for c in gains:
            c.wait()
        g_sum = g_a[0]
        for i in range(1, INNER):
            g_sum = g_sum + g_a[i]
        gain_acc[...] = g_sum
        g_b[ib] = g_sum
        gains = [remote_copy(gain_acc, g_b.at[ib], outer_peer(i)) for i in range(1, outer)]
        edge_sum.start_c()
    for k in (1, 4):
        rets[k].wait()
    n_base[...] += mm(onehot[1], ret_in[1]) + mm(onehot[4], ret_in[4])
    if fused:
        edge_sum.start_d()
    if fused:
        node_sum.finish()
    for k in (2, 5):
        rets[k].wait()
    total = n_base[...] + mm(onehot[2], ret_in[2]) + mm(onehot[5], ret_in[5])
    ngrad_ref[...] = total.astype(BF16)
    if fused:
        for c in gains:
            c.wait()
        g_sum = g_b[0]
        for i in range(1, outer):
            g_sum = g_sum + g_b[i]
        egain_out[...] = g_sum[0:1, :] * edge_scale
        ngain_out[...] = g_sum[8:9, :] * node_scale
        edge_sum.finish()
    else:
        egain_out[...] = gain_acc[0:1, :] * edge_scale
        ngain_out[...] = gain_acc[8:9, :] * node_scale
        give_weights(edge_sum.outs, lambda a, b: egw_ref[a:b, :] * edge_scale)
        give_weights(node_sum.outs, lambda a, b: ngw_ref[a:b, :] * node_scale)


def on_device(
    node_latent,
    agg_saved,
    node_cot,
    edge_latent,
    edge_cot,
    send_local,
    recv_local,
    send_slot,
    recv_slot,
    tile_count,
    edge_w_in,
    edge_w_out,
    edge_gain,
    node_w_in,
    node_w_out,
    node_gain,
):
    nb, h = node_latent.shape
    edges = edge_latent.shape[0]
    tile_total, tile = send_local.shape
    n = lax.axis_size("row")
    stride = n // 8
    node_scale = (nb * n) ** (-0.5)
    edge_scale = (edges * n) ** (-0.5)
    outer = n // INNER
    fused = n % INNER == 0 and 3 * h % (INNER * outer * 16) == 0 and 4 * h % (INNER * outer * 16) == 0
    levels = outer if fused else 2
    group = 4 * tile
    weights = 7 * h
    vmem = pl.BlockSpec(memory_space=pltpu.VMEM)
    smem = pl.BlockSpec(memory_space=pltpu.SMEM)
    copies = 20 + (2 * (2 * (INNER - 1) + 2 * (outer - 1)) + INNER - 1 + outer - 1 if fused else 0)
    anywhere = pl.BlockSpec(memory_space=pl.ANY)
    summed = BF16 if fused else F32
    node_grad, edge_grad, *sums = pl.pallas_call(
        functools.partial(layer_kernel, n, stride, fused, node_scale, edge_scale),
        out_shape=(
            jax.ShapeDtypeStruct((nb, h), BF16),
            jax.ShapeDtypeStruct((edges, h), BF16),
            jax.ShapeDtypeStruct((3 * h, h), summed),
            jax.ShapeDtypeStruct((h, h), summed),
            jax.ShapeDtypeStruct((2 * h, h), summed),
            jax.ShapeDtypeStruct((h, h), summed),
            jax.ShapeDtypeStruct((1, h), F32),
            jax.ShapeDtypeStruct((1, h), F32),
        ),
        in_specs=[anywhere] * 7 + [smem] * 3 + [anywhere] * 6,
        out_specs=(vmem,) * 8,
        scratch_shapes=[
            pltpu.VMEM((nb, h), BF16),
            pltpu.VMEM((nb, h), BF16),
            pltpu.VMEM((nb, h), BF16),
            pltpu.VMEM((edges, h), BF16),
            pltpu.VMEM((edges, h), BF16),
            pltpu.VMEM((tile_total, tile), jnp.int32),
            pltpu.VMEM((tile_total, tile), jnp.int32),
            pltpu.VMEM((3 * h, h), BF16),
            pltpu.VMEM((h, h), BF16),
            pltpu.VMEM((1, h), F32),
            pltpu.VMEM((2 * h, h), BF16),
            pltpu.VMEM((h, h), BF16),
            pltpu.VMEM((1, h), F32),
            pltpu.VMEM((4 * h, h), F32),
            pltpu.VMEM((3 * h, h), F32),
            pltpu.SemaphoreType.DMA((13,)),
            pltpu.VMEM((6, 1, group), jnp.int32),
            pltpu.VMEM((6, 1, group), jnp.int32),
            pltpu.VMEM((6, nb, group), BF16),
            pltpu.VMEM((6, group, h), BF16),
            pltpu.VMEM((6, group, h), BF16),
            pltpu.VMEM((3, group, h), BF16),
            pltpu.VMEM((3, group, h), BF16),
            pltpu.VMEM((6, group, h), BF16),
            pltpu.VMEM((6, group, h), BF16),
            pltpu.VMEM((nb, h), BF16),
            pltpu.VMEM((nb, h), BF16),
            pltpu.VMEM((nb, h), BF16),
            pltpu.VMEM((nb, h), BF16),
            pltpu.VMEM((nb, h), F32),
            pltpu.VMEM((edges, h), BF16),
            pltpu.VMEM((edges, h), BF16),
            pltpu.VMEM((edges, h), F32),
            pltpu.VMEM((edges, h), BF16),
            pltpu.VMEM((edges, h), F32),
            pltpu.VMEM((edges, h), BF16),
            pltpu.VMEM((edges, h), BF16),
            pltpu.VMEM((16, h), F32),
            pltpu.VMEM((weights, h), BF16),
            pltpu.VMEM((INNER - 1, weights // INNER, h), BF16),
            pltpu.VMEM((weights // INNER, h), F32),
            pltpu.VMEM((weights // INNER, h), BF16),
            pltpu.VMEM((levels - 1, weights // INNER // levels, h), BF16),
            pltpu.VMEM((weights, h), BF16),
            pltpu.VMEM((INNER, 16, h), F32),
            pltpu.VMEM((levels, 16, h), F32),
            pltpu.VMEM((3, group, h), BF16),
            pltpu.SemaphoreType.DMA((copies,)),
            pltpu.SemaphoreType.DMA((copies,)),
        ],
        compiler_params=pltpu.CompilerParams(
            collective_id=0, has_side_effects=True, vmem_limit_bytes=60 * 1024 * 1024
        ),
        cost_estimate=pl.CostEstimate(flops=7 * 10**9, bytes_accessed=8 * 10**6, transcendentals=10**6),
    )(
        node_latent,
        agg_saved,
        node_cot,
        edge_latent,
        edge_cot,
        send_local,
        recv_local,
        send_slot,
        recv_slot,
        tile_count,
        edge_w_in,
        edge_w_out,
        edge_gain[None, :],
        node_w_in,
        node_w_out,
        node_gain[None, :],
    )
    if not fused:
        sums = lax.psum(tuple(sums), "row")
    egwi, egwo, ngwi, ngwo, egain, ngain = [v.astype(F32) for v in sums]
    return (node_grad, edge_grad, egwi, egwo, egain[0], ngwi, ngwo, ngain[0])


def solution(mesh):
    placed = (P(("parts", "row"), None),) * 7 + (P(("parts", "row")),) * 3 + (P(),) * 6
    return jax.shard_map(
        on_device,
        mesh=mesh,
        in_specs=placed,
        out_specs=(
            P(("parts", "row"), None),
            P(("parts", "row"), None),
            P("parts", None),
            P("parts", None),
            P("parts"),
            P("parts", None),
            P("parts", None),
            P("parts"),
        ),
        check_vma=False,
    )
```
